512 devices in a mesh: row: 32 (over y_lo, z, core), col: 16 (over x, y_hi).
Axes of the slice: x: 4, y: 8 (y_hi: 4, y_lo: 2; y = y_hi * 2 + y_lo), z: 8, core: 2. Of those that a mesh axis runs over, the one named last changes fastest.
Arguments:
- inputs: bfloat16 [512, 12288], P('col', 'row'), may hold values from -6 to 6
- out_grad: bfloat16 [512, 12288], P('col', 'row'), may hold values from -5 to 5
- w_in: bfloat16 [12288, 24576], P('row', 'col'), may hold values from -0.0546875 to 0.0546875
- w_out: bfloat16 [24576, 12288], P('col', 'row'), may hold values from -0.0390625 to 0.0390625
Outputs:
- grad_inputs: bfloat16 [512, 12288], P('col', 'row')
- grad_w_in: bfloat16 [12288, 24576], P('row', 'col')
- grad_w_out: bfloat16 [24576, 12288], P('col', 'row')
The draws below stay inside these ranges and needn't reach their ends.
All inputs are finite; a program needn't handle non-finite values.
Results may differ from the reference program's by a relative error of at most 0.0049.
Values may be sent and summed in bfloat16 or wider, within the bound.
A program may use at most 64 MiB of HBM per device.

```python
import jax
import jax.numpy as jnp

D = 12288
F = 24576
TOKENS = 512


def strengthened(entries, rng, source, target, shards_of, factor):
    owner, partner = [(jnp.arange(entries.shape[axis_at]) // (entries.shape[axis_at] // shards_of)).reshape([-1 if axis == axis_at else 1 for axis in range(entries.ndim)]) for axis_at in (source, target)]
    chosen = jax.random.permutation(rng, shards_of)[partner]
    strong = (owner == chosen) | (owner == (partner + shards_of // 2) % shards_of)
    return jnp.where(strong, factor * entries, entries)


def shard_levels(rng, extent, pieces, least, top_value):
    level = 1.0
    for axis_at, shards_of in pieces:
        steps = jax.random.uniform(jax.random.fold_in(jax.random.fold_in(rng, 6), axis_at), (shards_of,), jnp.float32, least / len(pieces), top_value / len(pieces))
        level = level * jnp.repeat(jnp.exp(steps), extent[axis_at] // shards_of).reshape((-1,) + (1,) * (len(extent) - 1 - axis_at))
    return level


def gaussian(stream_key, extent, scale, bound, cuts=(), kind=jnp.bfloat16):
    drawn = jax.random.normal(stream_key, extent, jnp.float32) * scale
    if len(cuts) > 0:
        drawn = shard_levels(stream_key, extent, cuts, -0.22, 0.18) * drawn
    return jnp.clip(drawn, min=-bound, max=bound).astype(kind)


def gaussian_with(key, shape, deviation, limit, pieces, heavy, held_as=jnp.bfloat16):
    values = deviation * jax.random.normal(key, shape, jnp.float32)
    if pieces:
        values = values * shard_levels(key, shape, pieces, -0.22, 0.18)
    return jnp.clip(strengthened(values, jax.random.fold_in(key, 3), *heavy), -limit, limit).astype(held_as)


def setup_inputs(seed: int = 0) -> dict:
    keys = jax.random.split(jax.random.key(seed), 5)
    inputs = gaussian_with(keys[0], (TOKENS, D), 1.0, 6.0, ((0, 16), (1, 32)), (1, 0, 32, 2.75))
    out_grad = gaussian_with(keys[1], (TOKENS, D), (4 / TOKENS ** 0.5), 5.0, ((0, 16), (1, 32)), (1, 0, 32, 2.75))
    w_in = gaussian(keys[2], (D, F), D ** -0.5, 0.0546875, ((0, 32), (1, 16)))
    w_out = gaussian(keys[3], (F, D), F ** -0.5, 0.0390625, ((0, 16), (1, 32)))
    return dict(inputs=inputs, out_grad=out_grad, w_in=w_in, w_out=w_out)


slope_const = 0.7978845608028654
cubic_coef = 0.044715


def gelu_value(v):
    inner = slope_const * (v + cubic_coef * v * v * v)
    return 0.5 * v * (1.0 + jnp.tanh(inner))


def gelu_slope(v):
    inner = slope_const * (v + cubic_coef * v * v * v)
    tanh_val = jnp.tanh(inner)
    deriv = slope_const * (1.0 + 3.0 * cubic_coef * v * v)
    return 0.5 * (1.0 + tanh_val) + 0.5 * v * (1.0 - tanh_val * tanh_val) * deriv


def reference(inputs, out_grad, w_in, w_out):
    preact = jnp.dot(inputs, w_in, preferred_element_type=jnp.float32)
    upstream = jnp.dot(out_grad, w_out.T, preferred_element_type=jnp.float32)
    activation = gelu_value(preact).astype(jnp.bfloat16)
    hidden_grad = (upstream * gelu_slope(preact)).astype(jnp.bfloat16)
    grad_w_out = jnp.dot(activation.T, out_grad, preferred_element_type=jnp.float32).astype(jnp.bfloat16)
    grad_w_in = jnp.dot(inputs.T, hidden_grad, preferred_element_type=jnp.float32).astype(jnp.bfloat16)
    grad_inputs = jnp.dot(hidden_grad, w_in.T, preferred_element_type=jnp.float32).astype(jnp.bfloat16)
    return grad_inputs, grad_w_in, grad_w_out
```

```python
import functools

import jax
import jax.numpy as jnp
from jax import lax
from jax.experimental import pallas as pl
from jax.experimental.pallas import tpu as pltpu
from jax.sharding import PartitionSpec as P

MESH = pl.DeviceIdType.MESH
BF16 = jnp.bfloat16
F32 = jnp.float32

slope_const = 0.7978845608028654
cubic_coef = 0.044715

NX, NYH, NYL, NZ = 4, 4, 2, 8
TOKENS = 512
BLOCK = TOKENS // NX
PIECE = BLOCK // NYH
CHUNK = BLOCK // NZ
WIDTH = 384
HIDDEN = 1536
HALF = HIDDEN // 2


def nt(left, right):
    return lax.dot_general(
        left, right, (((1,), (1,)), ((), ())), preferred_element_type=F32
    )


def tn(left, right):
    return lax.dot_general(
        left, right, (((0,), (0,)), ((), ())), preferred_element_type=F32
    )


def activate(preact, upstream):
    square = preact * preact
    inner = slope_const * (preact + cubic_coef * square * preact)
    tanh_val = jnp.tanh(inner)
    deriv = slope_const * (1.0 + 3.0 * cubic_coef * square)
    value = 0.5 * preact * (1.0 + tanh_val)
    slope = 0.5 * (1.0 + tanh_val) + 0.5 * preact * (1.0 - tanh_val * tanh_val) * deriv
    return value.astype(BF16), (upstream * slope).astype(BF16)


def kernel(
    inputs, out_grad, w_in, w_out,
    grad_inputs, grad_w_in, grad_w_out,
    panel, wi, wo, w_full, part, rs_out, rs_in, y_out, y_in, ah,
    x_out, x_in, gx, gy_out, gy_in, gi_stage, gwi_stage, gwo_stage,
    local_sem, core_s, core_r, wx_s, wx_r, ys_s, ys_r, xs_s, xs_r, xf_s, xf_r,
    rs_s, rs_r, ye_s, ye_r, ag_s, ag_r, cf_s, cf_r, gx_s, gx_r, gy_s, gy_r,
):
    row, col = lax.axis_index("row"), lax.axis_index("col")
    y_lo, z, core = row // 16, (row // 2) % 8, row % 2
    x, y_hi = col // 4, col % 4
    other = 1 - core

    def device(y_lo=y_lo, z=z, core=core, x=x, y_hi=y_hi):
        return ((y_lo * NZ + z) * 2 + core, x * NYH + y_hi)

    twin = device(core=other)
    partner = device(y_lo=1 - y_lo)
    z_next = (device(z=(z + 1) % NZ), device(z=(z + NZ - 1) % NZ))
    x_next = (device(x=(x + 1) % NX), device(x=(x + NX - 1) % NX))
    x_far = device(x=(x + 2) % NX)
    y_peer = [device(y_hi=(y_hi + j + 1) % NYH) for j in range(3)]

    def remote(src, dst, send, recv, to):
        return pltpu.make_async_remote_copy(
            src_ref=src, dst_ref=dst, send_sem=send, recv_sem=recv,
            device_id=to, device_id_type=MESH,
        )

    def at16(start, size):
        return pl.ds(pl.multiple_of(start, 16), size)

    my_rows = at16(x * BLOCK + y_hi * PIECE, PIECE)
    half_cols = pl.ds(pl.multiple_of(core * HALF, 128), HALF)
    other_cols = pl.ds(pl.multiple_of(other * HALF, 128), HALF)
    own = [
        pltpu.make_async_copy(inputs, panel.at[0, my_rows, 0:WIDTH], local_sem.at[0]),
        pltpu.make_async_copy(out_grad, panel.at[1, my_rows, 0:WIDTH], local_sem.at[1]),
        pltpu.make_async_copy(w_in.at[:, half_cols], wi.at[0:WIDTH, :], local_sem.at[2]),
        pltpu.make_async_copy(w_out.at[half_cols, :], wo.at[:, 0:WIDTH], local_sem.at[3]),
        pltpu.make_async_copy(w_in, w_full, local_sem.at[4]),
    ]
    for copy in own:
        copy.start()

    barrier = pltpu.get_barrier_semaphore()
    greeted = [twin, partner, *z_next, *x_next, x_far, *y_peer]
    for peer in greeted:
        pl.semaphore_signal(barrier, inc=1, device_id=peer, device_id_type=MESH)
    pl.semaphore_wait(barrier, len(greeted))

    own[0].wait()
    own[1].wait()

    def piece_rows(block, j):
        return at16(block * BLOCK + ((y_hi + NYH - j) % NYH) * PIECE, PIECE)

    def to_twin(slot, rows):
        return remote(
            panel.at[:, rows, 0:WIDTH], panel.at[:, rows, WIDTH : 2 * WIDTH],
            core_s.at[slot], core_r.at[slot], twin,
        )

    def y_send(j):
        mine = panel.at[:, my_rows, 0:WIDTH]
        return remote(mine, mine, ys_s.at[j], ys_r.at[j], y_peer[j])

    def y_land(j):
        rows = panel.at[:, piece_rows(x, j + 1), 0:WIDTH]
        return remote(rows, rows, ys_s.at[j], ys_r.at[j], y_peer[j])

    def x_send(way, j):
        rows = panel.at[:, piece_rows(x, j), 0:WIDTH]
        return remote(rows, rows, xs_s.at[way, j], xs_r.at[way, j], x_next[way])

    def x_block(way):
        return (x + NX - 1) % NX if way == 0 else (x + 1) % NX

    def x_land(way, j):
        rows = panel.at[:, piece_rows(x_block(way), j), 0:WIDTH]
        return remote(rows, rows, xs_s.at[way, j], xs_r.at[way, j], x_next[way])

    def x_forward(way, j):
        rows = panel.at[way, piece_rows(x_block(way), j), 0:WIDTH]
        return remote(rows, rows, xf_s.at[way, j], xf_r.at[way, j], x_next[way])

    def x_forward_land(way, j):
        rows = panel.at[way, piece_rows((x + 2) % NX, j), 0:WIDTH]
        return remote(rows, rows, xf_s.at[way, j], xf_r.at[way, j], x_next[way])

    for j in range(3):
        y_send(j).start()
    for way in range(2):
        x_send(way, 0).start()
    to_twin(0, my_rows).start()
    w_swap = [
        remote(w_in.at[:, other_cols], wi.at[WIDTH : 2 * WIDTH, :], wx_s.at[0], wx_r.at[0], twin),
        remote(w_out.at[other_cols, :], wo.at[:, WIDTH : 2 * WIDTH], wx_s.at[1], wx_r.at[1], twin),
    ]
    for copy in w_swap:
        copy.start()
    for j in range(3):
        y_land(j).wait_recv()
        for way in range(2):
            x_send(way, j + 1).start()
        to_twin(j + 1, piece_rows(x, j + 1)).start()

    def block_of(k):
        step = jnp.where(k == 2, 3, jnp.where(k == 3, 2, k))
        return (x + step) % NX

    def matmuls(k):
        for j in range(4):
            slot = k * 4 + j
            rows = piece_rows(block_of(k), j)
            landed = panel.at[:, rows, WIDTH : 2 * WIDTH]
            remote(landed, landed, core_s.at[slot], core_r.at[slot], twin).wait_recv()
        rows = at16(block_of(k) * BLOCK, BLOCK)
        part[k, 0] = jnp.dot(panel[0, rows, :], wi[...], preferred_element_type=F32)
        part[k, 1] = nt(panel[1, rows, :], wo[...])

    def rs_copy(way, k, s):
        if s == 0:
            src, dst = rs_out.at[way, k, 0, way], rs_in.at[way, k, 0, way]
        else:
            src, dst = rs_out.at[way, k, s], rs_in.at[way, k, s]
        return remote(src, dst, rs_s.at[way, k, s], rs_r.at[way, k, s], z_next[way])

    def rs_step(k, s):
        for way in range(2):
            target = (z + NZ + (4 - s if way == 0 else s - 4)) % NZ
            rows = at16(target * CHUNK, CHUNK)
            if s > 0:
                rs_copy(way, k, s - 1).wait_recv()
            for array in range(2):
                if s == 0 and array != way:
                    continue
                term = part[k, array, rows, :]
                if s > 1 or (s == 1 and array == way):
                    term = term + rs_in[way, k, s - 1, array].astype(F32)
                rs_out[way, k, s, array] = term.astype(BF16)
            rs_copy(way, k, s).start()

    def y_exchange(k):
        return remote(y_out.at[k], y_in.at[k], ye_s.at[k], ye_r.at[k], partner)

    def rs_end(k):
        rows = at16(z * CHUNK, CHUNK)
        for way in range(2):
            rs_copy(way, k, 3).wait_recv()
        for array in range(2):
            y_out[k, array] = part[k, array, rows, :] + (
                rs_in[0, k, 3, array].astype(F32) + rs_in[1, k, 3, array].astype(F32)
            )
        y_exchange(k).start()

    def ag_copy(way, k, s, origin):
        rows = at16(block_of(k) * BLOCK + origin * CHUNK, CHUNK)
        ref = ah.at[core, way, rows, :] if s == 3 else ah.at[core, :, rows, :]
        return remote(ref, ref, ag_s.at[way, k, s], ag_r.at[way, k, s], z_next[way])

    def ag_origin(way, s):
        return (z + NZ + (-s if way == 0 else s)) % NZ

    def ag_step(k, s):
        for way in range(2):
            if s > 0:
                ag_copy(way, k, s - 1, ag_origin(way, s)).wait_recv()
            ag_copy(way, k, s, ag_origin(way, s)).start()

    def gelu(k):
        y_exchange(k).wait_recv()
        value, grad = activate(y_out[k, 0] + y_in[k, 0], y_out[k, 1] + y_in[k, 1])
        rows = at16(block_of(k) * BLOCK + z * CHUNK, CHUNK)
        ah[core, 0, rows, :] = value
        ah[core, 1, rows, :] = grad
        ag_step(k, 0)

    def half_swap(k, half):
        ref = ah.at[half, :, at16(block_of(k) * BLOCK, BLOCK), :]
        return remote(ref, ref, cf_s.at[k], cf_r.at[k], twin)

    def ag_end(k):
        for way in range(2):
            ag_copy(way, k, 3, ag_origin(way, 4)).wait_recv()
        half_swap(k, core).start()

    x_to = {1: x_next[0], 2: x_next[1], 3: x_far}

    def gx_copy(k):
        return remote(x_out.at[k - 1], x_in.at[k - 1], gx_s.at[k - 1], gx_r.at[k - 1], x_to[k])

    def grad_block(k):
        half_swap(k, other).wait_recv()
        rows = at16(block_of(k) * BLOCK, BLOCK)
        return nt(ah[0, 1, rows, :], w_full[:, 0:HALF]) + nt(
            ah[1, 1, rows, :], w_full[:, HALF:HIDDEN]
        )

    own[2].wait()
    own[3].wait()
    for copy in w_swap:
        copy.wait_recv()
    matmuls(0)
    rs_step(0, 0)
    for j in range(4):
        for way in range(2):
            x_land(way, j).wait_recv()
            x_forward(way, j).start()
            to_twin((1 if way == 1 else 2) * 4 + j, piece_rows(x_block(way), j)).start()
    rs_step(0, 1)
    matmuls(1)
    rs_step(1, 0)
    matmuls(2)
    rs_step(2, 0)
    for j in range(4):
        for way in range(2):
            x_forward_land(way, j).wait_recv()
        to_twin(12 + j, piece_rows((x + 2) % NX, j)).start()
    rs_step(0, 2)
    rs_step(1, 1)
    rs_step(2, 1)
    matmuls(3)
    rs_step(3, 0)
    rs_step(0, 3)
    rs_step(1, 2)
    rs_step(2, 2)
    rs_step(3, 1)
    rs_end(0)
    rs_step(1, 3)
    rs_step(2, 3)
    rs_step(3, 2)
    gelu(0)
    rs_end(1)
    rs_end(2)
    rs_step(3, 3)
    ag_step(0, 1)
    gelu(1)
    gelu(2)
    rs_end(3)
    ag_step(0, 2)
    ag_step(1, 1)
    ag_step(2, 1)
    gelu(3)
    ag_step(1, 2)
    ag_step(2, 2)
    ag_step(3, 1)
    ag_step(1, 3)
    ag_step(2, 3)
    ag_step(3, 2)
    ag_step(0, 3)
    ag_end(1)
    ag_end(2)
    ag_step(3, 3)
    ag_end(0)
    own[4].wait()
    for k in (1, 2):
        x_out[k - 1] = grad_block(k)
        gx_copy(k).start()
    ag_end(3)
    gx[...] = grad_block(0)
    x_out[2] = grad_block(3)
    gx_copy(3).start()

    def gwo_part(half):
        rows = pl.ds(half * HALF, HALF)
        gwo_stage[rows, :] = tn(ah[half, 0], panel[1, :, 0:WIDTH]).astype(BF16)
        copy = pltpu.make_async_copy(
            gwo_stage.at[rows, :], grad_w_out.at[rows, :], local_sem.at[5 + half]
        )
        copy.start()
        return copy

    def gwi_part(half):
        cols = pl.ds(half * HALF, HALF)
        gwi_stage[:, cols] = tn(panel[0, :, 0:WIDTH], ah[half, 1]).astype(BF16)
        copy = pltpu.make_async_copy(
            gwi_stage.at[:, cols], grad_w_in.at[:, cols], local_sem.at[7 + half]
        )
        copy.start()
        return copy

    written = [gwo_part(0), gwo_part(1)]
    for k in (1, 2, 3):
        gx_copy(k).wait_recv()
        gx[...] += x_in[k - 1]

    def gy_copy(j):
        return remote(gy_out.at[j], gy_in.at[j], gy_s.at[j], gy_r.at[j], y_peer[j])

    for j in range(3):
        gy_out[j] = gx[at16(((y_hi + j + 1) % NYH) * PIECE, PIECE), :]
        gy_copy(j).start()
    written += [gwi_part(0), gwi_part(1)]
    total = gx[at16(y_hi * PIECE, PIECE), :]
    for j in range(3):
        gy_copy(j).wait_recv()
        total = total + gy_in[j]
    gi_stage[...] = total.astype(BF16)
    last = pltpu.make_async_copy(gi_stage, grad_inputs, local_sem.at[9])
    last.start()

    for j in range(3):
        y_send(j).wait_send()
        gy_copy(j).wait_send()
    for way in range(2):
        for j in range(4):
            x_send(way, j).wait_send()
            x_forward(way, j).wait_send()
    for k in range(4):
        for j in range(4):
            to_twin(k * 4 + j, piece_rows(block_of(k), j)).wait_send()
        for s in range(4):
            for way in range(2):
                rs_copy(way, k, s).wait_send()
                ag_copy(way, k, s, ag_origin(way, s)).wait_send()
        y_exchange(k).wait_send()
        half_swap(k, core).wait_send()
    for k in (1, 2, 3):
        gx_copy(k).wait_send()
    for copy in w_swap:
        copy.wait_send()
    for copy in written:
        copy.wait()
    last.wait()


def body(inputs, out_grad, w_in, w_out):
    any_space = pl.BlockSpec(memory_space=pl.ANY)
    dma = pltpu.SemaphoreType.DMA
    return pl.pallas_call(
        kernel,
        out_shape=(
            jax.ShapeDtypeStruct((PIECE, WIDTH), BF16),
            jax.ShapeDtypeStruct((WIDTH, HIDDEN), BF16),
            jax.ShapeDtypeStruct((HIDDEN, WIDTH), BF16),
        ),
        in_specs=[any_space] * 4,
        out_specs=(any_space,) * 3,
        scratch_shapes=[
            pltpu.VMEM((2, TOKENS, 2 * WIDTH), BF16),
            pltpu.VMEM((2 * WIDTH, HALF), BF16),
            pltpu.VMEM((HALF, 2 * WIDTH), BF16),
            pltpu.VMEM((WIDTH, HIDDEN), BF16),
            pltpu.VMEM((4, 2, BLOCK, HALF), F32),
            pltpu.VMEM((2, 4, 4, 2, CHUNK, HALF), BF16),
            pltpu.VMEM((2, 4, 4, 2, CHUNK, HALF), BF16),
            pltpu.VMEM((4, 2, CHUNK, HALF), F32),
            pltpu.VMEM((4, 2, CHUNK, HALF), F32),
            pltpu.VMEM((2, 2, TOKENS, HALF), BF16),
            pltpu.VMEM((3, BLOCK, WIDTH), F32),
            pltpu.VMEM((3, BLOCK, WIDTH), F32),
            pltpu.VMEM((BLOCK, WIDTH), F32),
            pltpu.VMEM((3, PIECE, WIDTH), F32),
            pltpu.VMEM((3, PIECE, WIDTH), F32),
            pltpu.VMEM((PIECE, WIDTH), BF16),
            pltpu.VMEM((WIDTH, HIDDEN), BF16),
            pltpu.VMEM((HIDDEN, WIDTH), BF16),
            dma((10,)),
            dma((16,)), dma((16,)),
            dma((2,)), dma((2,)),
            dma((3,)), dma((3,)),
            dma((2, 4)), dma((2, 4)),
            dma((2, 4)), dma((2, 4)),
            dma((2, 4, 4)), dma((2, 4, 4)),
            dma((4,)), dma((4,)),
            dma((2, 4, 4)), dma((2, 4, 4)),
            dma((4,)), dma((4,)),
            dma((3,)), dma((3,)),
            dma((3,)), dma((3,)),
        ],
        compiler_params=pltpu.CompilerParams(
            collective_id=0, has_side_effects=True, vmem_limit_bytes=40 << 20
        ),
        cost_estimate=pl.CostEstimate(
            flops=6 * 10**9, bytes_accessed=5 * 10**6, transcendentals=10**6
        ),
        name="ffn_backward",
    )(inputs, out_grad, w_in, w_out)


def solution(mesh):
    return jax.shard_map(
        body,
        mesh=mesh,
        in_specs=(P("col", "row"), P("col", "row"), P("row", "col"), P("col", "row")),
        out_specs=(P("col", "row"), P("row", "col"), P("col", "row")),
        check_vma=False,
    )
```

```python
import functools

import jax
import jax.numpy as jnp
from jax import lax
from jax.experimental import pallas as pl
from jax.experimental.pallas import tpu as pltpu
from jax.sharding import PartitionSpec as P

MESH = pl.DeviceIdType.MESH
BF16 = jnp.bfloat16
F32 = jnp.float32

slope_const = 0.7978845608028654
cubic_coef = 0.044715

NX, NYH, NYL, NZ = 4, 4, 2, 8
TOKENS = 512
BLOCK = TOKENS // 4
PIECE = TOKENS // (NX * NYH)
CHUNK = BLOCK // NZ
WIDTH = 384
HIDDEN = 1536
HALF = HIDDEN // 2

DY = (0, 1, 3, 2)

SEMAPHORES = {
    "core": (4, 4),
    "wx": (2,),
    "ys": (3,),
    "xs": (3, 4),
    "rs": (2, 4, 4),
    "ye": (4,),
    "ag": (2, 4, 4),
    "cf": (4,),
    "gx": (3, 4),
    "gy": (3,),
}


def nt(left, right):
    return lax.dot_general(
        left, right, (((1,), (1,)), ((), ())), preferred_element_type=F32
    )


def tn(left, right):
    return lax.dot_general(
        left, right, (((0,), (0,)), ((), ())), preferred_element_type=F32
    )


def activate(preact, upstream):
    square = preact * preact
    inner = slope_const * (preact + cubic_coef * square * preact)
    tanh_val = jnp.tanh(inner)
    deriv = slope_const * (1.0 + 3.0 * cubic_coef * square)
    value = 0.5 * preact * (1.0 + tanh_val)
    slope = 0.5 * (1.0 + tanh_val) + 0.5 * preact * (1.0 - tanh_val * tanh_val) * deriv
    return value.astype(BF16), (upstream * slope).astype(BF16)


def kernel(
    inputs, out_grad, w_in, w_out,
    grad_inputs, grad_w_in, grad_w_out,
    panel, wi, wo, w_full, wo_other, part, rs_out, rs_in, y_out, y_in, ah,
    g, gx_in, gy_out, gy_in, local_sem, *pairs,
):
    row, col = lax.axis_index("row"), lax.axis_index("col")
    y_lo, z, core = row // 16, (row // 2) % 8, row % 2
    x, y_hi = col // 4, col % 4
    other = 1 - core

    def device(y_lo=y_lo, z=z, core=core, x=x, y_hi=y_hi):
        return ((y_lo * NZ + z) * 2 + core, x * NYH + y_hi)

    twin = device(core=other)
    partner = device(y_lo=1 - y_lo)
    z_next = (device(z=(z + 1) % NZ), device(z=(z + NZ - 1) % NZ))
    x_peer = [None, *(device(x=(x + d) % NX) for d in range(1, NX))]
    y_peer = [None, *(device(y_hi=(y_hi + d) % NYH) for d in range(1, NYH))]

    sems = {kind: pairs[2 * i : 2 * i + 2] for i, kind in enumerate(SEMAPHORES)}
    sent = []

    def remote(src, dst, kind, index, to):
        send, recv = sems[kind]
        return pltpu.make_async_remote_copy(
            src_ref=src, dst_ref=dst, send_sem=send.at[index], recv_sem=recv.at[index],
            device_id=to, device_id_type=MESH,
        )

    def start(copy):
        copy.start()
        sent.append(copy)

    half_cols = pl.ds(pl.multiple_of(core * HALF, 128), HALF)
    other_cols = pl.ds(pl.multiple_of(other * HALF, 128), HALF)
    own = [
        pltpu.make_async_copy(inputs, panel.at[0, 0:PIECE, 0:WIDTH], local_sem.at[0]),
        pltpu.make_async_copy(out_grad, panel.at[1, 0:PIECE, 0:WIDTH], local_sem.at[1]),
        pltpu.make_async_copy(w_in.at[:, half_cols], wi.at[0:WIDTH, :], local_sem.at[2]),
        pltpu.make_async_copy(w_out.at[half_cols, :], wo.at[:, 0:WIDTH], local_sem.at[3]),
        pltpu.make_async_copy(w_in, w_full, local_sem.at[4]),
        pltpu.make_async_copy(w_out.at[other_cols, :], wo_other, local_sem.at[5]),
    ]
    for copy in own:
        copy.start()

    barrier = pltpu.get_barrier_semaphore()
    greeted = [twin, partner, *z_next, *x_peer[1:], *y_peer[1:]]
    for peer in greeted:
        pl.semaphore_signal(barrier, inc=1, device_id=peer, device_id_type=MESH)
    pl.semaphore_wait(barrier, len(greeted))

    def piece_rows(dx, dy):
        slot = 4 * DY.index(dy) + dx
        return slice(slot * PIECE, (slot + 1) * PIECE)

    def piece(dx, dy):
        return panel.at[:, piece_rows(dx, dy), 0:WIDTH]

    def to_twin(dx, dy):
        there = panel.at[:, piece_rows(dx, dy), WIDTH : 2 * WIDTH]
        return remote(piece(dx, dy), there, "core", (dx, dy), twin)

    def y_copy(d):
        return remote(piece(0, 0), piece(0, NYH - d), "ys", (d - 1,), y_peer[d])

    def x_copy(d, dy):
        return remote(piece(0, dy), piece(NX - d, dy), "xs", (d - 1, dy), x_peer[d])

    def own_ready(dy):
        for d in (1, 3, 2):
            start(x_copy(d, dy))
        start(to_twin(0, dy))

    def y_arrive(d):
        y_copy(d).wait_recv()
        own_ready(NYH - d)

    def x_arrive(dy):
        for d in (1, 3, 2):
            x_copy(d, dy).wait_recv()
            start(to_twin(NX - d, dy))

    def matmuls(k):
        for dx in range(NX):
            to_twin(dx, DY[k]).wait_recv()
        rows = slice(k * BLOCK, (k + 1) * BLOCK)
        part[k, 0] = jnp.dot(panel[0, rows, :], wi[...], preferred_element_type=F32)
        part[k, 1] = nt(panel[1, rows, :], wo[...])

    def chunk(start):
        return pl.ds(pl.multiple_of(start, 16), CHUNK)

    def rs_copy(way, k, s):
        if s == 0:
            src, dst = rs_out.at[way, k, 0, way], rs_in.at[way, k, 0, way]
        else:
            src, dst = rs_out.at[way, k, s], rs_in.at[way, k, s]
        return remote(src, dst, "rs", (way, k, s), z_next[way])

    def rs_step(k, s):
        for way in range(2):
            target = (z + NZ + (4 - s if way == 0 else s - 4)) % NZ
            rows = chunk(target * CHUNK)
            if s > 0:
                rs_copy(way, k, s - 1).wait_recv()
            for array in range(2):
                if s == 0 and array != way:
                    continue
                term = part[k, array, rows, :]
                if s > 1 or (s == 1 and array == way):
                    term = term + rs_in[way, k, s - 1, array].astype(F32)
                rs_out[way, k, s, array] = term.astype(BF16)
            start(rs_copy(way, k, s))

    def y_exchange(k):
        return remote(y_out.at[k], y_in.at[k], "ye", (k,), partner)

    def rs_end(k):
        rows = chunk(z * CHUNK)
        for way in range(2):
            rs_copy(way, k, 3).wait_recv()
        for array in range(2):
            y_out[k, array] = part[k, array, rows, :] + (
                rs_in[0, k, 3, array].astype(F32) + rs_in[1, k, 3, array].astype(F32)
            )
        start(y_exchange(k))

    def ag_copy(way, k, s, origin):
        rows = chunk(k * BLOCK + origin * CHUNK)
        ref = ah.at[core, way, rows, :] if s == 3 else ah.at[core, :, rows, :]
        return remote(ref, ref, "ag", (way, k, s), z_next[way])

    def ag_origin(way, s):
        return (z + NZ + (-s if way == 0 else s)) % NZ

    def ag_step(k, s):
        for way in range(2):
            if s > 0:
                ag_copy(way, k, s - 1, ag_origin(way, s)).wait_recv()
            start(ag_copy(way, k, s, ag_origin(way, s)))

    def gelu(k):
        y_exchange(k).wait_recv()
        value, grad = activate(y_out[k, 0] + y_in[k, 0], y_out[k, 1] + y_in[k, 1])
        rows = chunk(k * BLOCK + z * CHUNK)
        ah[core, 0, rows, :] = value
        ah[core, 1, rows, :] = grad
        ag_step(k, 0)

    def half_swap(k, half):
        ref = ah.at[half, :, k * BLOCK : (k + 1) * BLOCK, :]
        return remote(ref, ref, "cf", (k,), twin)

    def ag_end(k):
        for way in range(2):
            ag_copy(way, k, 3, ag_origin(way, 4)).wait_recv()
        start(half_swap(k, core))

    def g_piece(dx, dy):
        return g.at[DY.index(dy), dx * PIECE : (dx + 1) * PIECE]

    def gx_copy(dx, dy):
        return remote(g_piece(dx, dy), gx_in.at[dx - 1, dy], "gx", (dx - 1, dy), x_peer[dx])

    def grad_block(k):
        half_swap(k, other).wait_recv()
        rows = slice(k * BLOCK, (k + 1) * BLOCK)
        g[k] = nt(ah[0, 1, rows, :], w_full[:, 0:HALF]) + nt(
            ah[1, 1, rows, :], w_full[:, HALF:HIDDEN]
        )
        for dx in (2, 1, 3):
            start(gx_copy(dx, DY[k]))

    def x_sum(dy):
        total = g_piece(0, dy)[...]
        for dx in range(1, NX):
            gx_copy(dx, dy).wait_recv()
            total = total + gx_in[dx - 1, dy]
        return total

    def gy_copy(dy):
        return remote(gy_out.at[dy - 1], gy_in.at[dy - 1], "gy", (dy - 1,), y_peer[dy])

    def y_part(dy):
        gy_out[dy - 1] = x_sum(dy)
        start(gy_copy(dy))

    def weight_grads(half):
        cols = slice(half * HALF, (half + 1) * HALF)
        grad_w_out[cols, :] = tn(ah[half, 0], panel[1, :, 0:WIDTH]).astype(BF16)
        grad_w_in[:, cols] = tn(panel[0, :, 0:WIDTH], ah[half, 1]).astype(BF16)

    own[0].wait()
    own[1].wait()
    for d in (1, 3, 2):
        start(y_copy(d))
    own_ready(0)
    own[4].wait()
    own[5].wait()
    w_swap = [
        remote(w_full.at[:, other_cols], wi.at[WIDTH : 2 * WIDTH, :], "wx", (0,), twin),
        remote(wo_other, wo.at[:, WIDTH : 2 * WIDTH], "wx", (1,), twin),
    ]
    for copy in w_swap:
        start(copy)
    own[2].wait()
    own[3].wait()
    x_arrive(0)
    y_arrive(1)
    y_arrive(3)
    for copy in w_swap:
        copy.wait_recv()
    matmuls(0)
    rs_step(0, 0)
    y_arrive(2)
    rs_step(0, 1)
    x_arrive(3)
    matmuls(2)
    x_arrive(1)
    rs_step(2, 0)
    matmuls(1)
    x_arrive(2)
    rs_step(1, 0)
    rs_step(0, 2)
    rs_step(2, 1)
    matmuls(3)
    rs_step(3, 0)
    rs_step(1, 1)
    rs_step(0, 3)
    rs_step(2, 2)
    rs_step(3, 1)
    rs_step(1, 2)
    rs_end(0)
    rs_step(2, 3)
    rs_step(3, 2)
    rs_step(1, 3)
    rs_end(2)
    gelu(0)
    rs_step(3, 3)
    rs_end(1)
    ag_step(0, 1)
    gelu(2)
    rs_end(3)
    gelu(1)
    ag_step(0, 2)
    ag_step(2, 1)
    gelu(3)
    ag_step(1, 1)
    ag_step(0, 3)
    ag_step(2, 2)
    ag_step(3, 1)
    ag_step(1, 2)
    ag_end(0)
    ag_step(2, 3)
    grad_block(0)
    ag_step(3, 2)
    ag_step(1, 3)
    ag_end(2)
    ag_step(3, 3)
    grad_block(2)
    ag_end(1)
    grad_block(1)
    ag_end(3)
    grad_block(3)
    y_part(3)
    weight_grads(0)
    weight_grads(1)
    y_part(1)
    y_part(2)
    total = x_sum(0)
    for dy in range(1, NYH):
        gy_copy(dy).wait_recv()
        total = total + gy_in[dy - 1]
    grad_inputs[...] = total.astype(BF16)

    for copy in sent:
        copy.wait_send()


def store(*refs):
    half = len(refs) // 2
    sems = refs[-1]
    copies = [
        pltpu.make_async_copy(refs[i], refs[half + i], sems.at[i]) for i in range(half)
    ]
    for copy in copies:
        copy.start()
    for copy in copies:
        copy.wait()


def body(inputs, out_grad, w_in, w_out):
    hbm = pl.BlockSpec(memory_space=pltpu.HBM)
    vmem = pl.BlockSpec(memory_space=pltpu.VMEM)
    dma = pltpu.SemaphoreType.DMA
    shapes = ((PIECE, WIDTH), (WIDTH, HIDDEN), (HIDDEN, WIDTH))
    results = pl.pallas_call(
        kernel,
        out_shape=tuple(pltpu.VMEM(shape, BF16) for shape in shapes),
        in_specs=[hbm] * 4,
        out_specs=(vmem,) * 3,
        scratch_shapes=[
            pltpu.VMEM((2, TOKENS, 2 * WIDTH), BF16),
            pltpu.VMEM((2 * WIDTH, HALF), BF16),
            pltpu.VMEM((HALF, 2 * WIDTH), BF16),
            pltpu.VMEM((WIDTH, HIDDEN), BF16),
            pltpu.VMEM((HALF, WIDTH), BF16),
            pltpu.VMEM((4, 2, BLOCK, HALF), F32),
            pltpu.VMEM((2, 4, 4, 2, CHUNK, HALF), BF16),
            pltpu.VMEM((2, 4, 4, 2, CHUNK, HALF), BF16),
            pltpu.VMEM((4, 2, CHUNK, HALF), F32),
            pltpu.VMEM((4, 2, CHUNK, HALF), F32),
            pltpu.VMEM((2, 2, TOKENS, HALF), BF16),
            pltpu.VMEM((4, BLOCK, WIDTH), F32),
            pltpu.VMEM((3, 4, PIECE, WIDTH), F32),
            pltpu.VMEM((3, PIECE, WIDTH), F32),
            pltpu.VMEM((3, PIECE, WIDTH), F32),
            dma((6,)),
            *(dma(shape) for shape in SEMAPHORES.values() for _ in range(2)),
        ],
        compiler_params=pltpu.CompilerParams(
            collective_id=0, has_side_effects=True, vmem_limit_bytes=60 << 20
        ),
        cost_estimate=pl.CostEstimate(
            flops=6 * 10**9, bytes_accessed=5 * 10**6, transcendentals=10**6
        ),
        name="ffn_backward",
    )(inputs, out_grad, w_in, w_out)
    return pl.pallas_call(
        store,
        out_shape=tuple(jax.ShapeDtypeStruct(shape, BF16) for shape in shapes),
        in_specs=[pl.BlockSpec(memory_space=pl.ANY)] * 3,
        out_specs=(pl.BlockSpec(memory_space=pl.ANY),) * 3,
        scratch_shapes=[dma((3,))],
        compiler_params=pltpu.CompilerParams(vmem_limit_bytes=1 << 20),
        name="store_results",
    )(*results)


def solution(mesh):
    return jax.shard_map(
        body,
        mesh=mesh,
        in_specs=(P("col", "row"), P("col", "row"), P("row", "col"), P("col", "row")),
        out_specs=(P("col", "row"), P("row", "col"), P("col", "row")),
        check_vma=False,
    )
```

```python
import functools

import jax
import jax.numpy as jnp
from jax import lax
from jax.experimental import pallas as pl
from jax.experimental.pallas import tpu as pltpu
from jax.sharding import PartitionSpec as P

MESH = pl.DeviceIdType.MESH
BF16 = jnp.bfloat16
F32 = jnp.float32

slope_const = 0.7978845608028654
cubic_coef = 0.044715

NX, NYH, NYL, NZ = 4, 4, 2, 8
TOKENS = 512
BLOCK = TOKENS // 4
PIECE = TOKENS // (NX * NYH)
CHUNK = BLOCK // NZ
WIDTH = 384
HIDDEN = 1536
HALF = HIDDEN // 2

DY = (0, 1, 3, 2)

SEMAPHORES = {
    "core": (2, 4, 4),
    "wx": (2,),
    "ys": (2, 2),
    "yf": (2,),
    "xs": (2, 3, 4),
    "rs": (2, 4, 4, 2),
    "ye": (4, 2),
    "ag": (2, 4, 4, 2),
    "cf": (4, 2),
    "gx": (3, 4),
    "gy": (3,),
}


def nt(left, right):
    return lax.dot_general(
        left, right, (((1,), (1,)), ((), ())), preferred_element_type=F32
    )


def tn(left, right):
    return lax.dot_general(
        left, right, (((0,), (0,)), ((), ())), preferred_element_type=F32
    )


def activate(preact, upstream):
    square = preact * preact
    inner = slope_const * (preact + cubic_coef * square * preact)
    tanh_val = jnp.tanh(inner)
    deriv = slope_const * (1.0 + 3.0 * cubic_coef * square)
    value = 0.5 * preact * (1.0 + tanh_val)
    slope = 0.5 * (1.0 + tanh_val) + 0.5 * preact * (1.0 - tanh_val * tanh_val) * deriv
    return value.astype(BF16), (upstream * slope).astype(BF16)


def kernel(
    inputs, out_grad, w_in, w_out,
    grad_inputs, grad_w_in, grad_w_out,
    panel, wi, wo, w_full, wo_other, part, rs_out, rs_in, y_out, y_in, ah,
    g, gx_in, gy_out, gy_in, g_sent, gy_far, local_sem, *pairs,
):
    row, col = lax.axis_index("row"), lax.axis_index("col")
    y_lo, z, core = row // 16, (row // 2) % 8, row % 2
    x, y_hi = col // 4, col % 4
    other = 1 - core

    def device(y_lo=y_lo, z=z, core=core, x=x, y_hi=y_hi):
        return ((y_lo * NZ + z) * 2 + core, x * NYH + y_hi)

    twin = device(core=other)
    partner = device(y_lo=1 - y_lo)
    z_next = (device(z=(z + 1) % NZ), device(z=(z + NZ - 1) % NZ))
    z_over = (device(z=(z + 2) % NZ), device(z=(z + NZ - 2) % NZ))
    x_peer = [None, *(device(x=(x + d) % NX) for d in range(1, NX))]
    y_peer = [None, *(device(y_hi=(y_hi + d) % NYH) for d in range(1, NYH))]

    sems = {kind: pairs[2 * i : 2 * i + 2] for i, kind in enumerate(SEMAPHORES)}
    sent = []

    def remote(src, dst, kind, index, to):
        send, recv = sems[kind]
        return pltpu.make_async_remote_copy(
            src_ref=src, dst_ref=dst, send_sem=send.at[index], recv_sem=recv.at[index],
            device_id=to, device_id_type=MESH,
        )

    def start(copy):
        copy.start()
        sent.append(copy)

    half_cols = pl.ds(pl.multiple_of(core * HALF, 128), HALF)
    other_cols = pl.ds(pl.multiple_of(other * HALF, 128), HALF)
    own = [
        pltpu.make_async_copy(inputs, panel.at[0, 0:PIECE, 0:WIDTH], local_sem.at[0]),
        pltpu.make_async_copy(out_grad, panel.at[1, 0:PIECE, 0:WIDTH], local_sem.at[1]),
        pltpu.make_async_copy(w_in.at[:, half_cols], wi.at[0:WIDTH, :], local_sem.at[2]),
        pltpu.make_async_copy(w_out.at[half_cols, :], wo.at[:, 0:WIDTH], local_sem.at[3]),
        pltpu.make_async_copy(w_in, w_full, local_sem.at[4]),
        pltpu.make_async_copy(w_out.at[other_cols, :], wo_other, local_sem.at[5]),
    ]
    for copy in own:
        copy.start()

    barrier = pltpu.get_barrier_semaphore()
    greeted = [twin, partner, *z_next, *z_over, *x_peer[1:], *y_peer[1:]]
    for peer in greeted:
        pl.semaphore_signal(barrier, inc=1, device_id=peer, device_id_type=MESH)
    pl.semaphore_wait(barrier, len(greeted))

    def piece_rows(dx, dy):
        slot = 4 * DY.index(dy) + dx
        return slice(slot * PIECE, (slot + 1) * PIECE)

    def piece(dx, dy, a):
        return panel.at[a, piece_rows(dx, dy), 0:WIDTH]

    def to_twin(dx, dy, a):
        there = panel.at[a, piece_rows(dx, dy), WIDTH : 2 * WIDTH]
        return remote(piece(dx, dy, a), there, "core", (a, dx, dy), twin)

    def y_copy(d, a):
        return remote(piece(0, 0, a), piece(0, NYH - d, a), "ys", (a, d // 2), y_peer[d])

    def y_forward(a):
        d = 1 if a == 0 else 3
        return remote(piece(0, NYH - d, a), piece(0, 2, a), "yf", (a,), y_peer[d])

    def x_copy(d, dy, a):
        return remote(piece(0, dy, a), piece(NX - d, dy, a), "xs", (a, d - 1, dy), x_peer[d])

    def own_ready(dy, a):
        for d in (1, 3, 2):
            start(x_copy(d, dy, a))
        start(to_twin(0, dy, a))

    def y_arrive(d, a):
        if d == 2:
            y_forward(a).wait_recv()
        else:
            y_copy(d, a).wait_recv()
            if d == (1 if a == 0 else 3):
                start(y_forward(a))
        own_ready(NYH - d, a)

    def x_arrive(dy, a):
        for d in (1, 3, 2):
            x_copy(d, dy, a).wait_recv()
            start(to_twin(NX - d, dy, a))

    def matmuls(k, a):
        for dx in range(NX):
            to_twin(dx, DY[k], a).wait_recv()
        rows = slice(k * BLOCK, (k + 1) * BLOCK)
        if a == 0:
            part[k, 0] = jnp.dot(panel[0, rows, :], wi[...], preferred_element_type=F32)
        else:
            part[k, 1] = nt(panel[1, rows, :], wo[...])

    def chunk(start):
        return pl.ds(pl.multiple_of(start, 16), CHUNK)

    def rs_copy(way, k, s, a):
        to = z_over[way] if s == 0 else z_next[way]
        return remote(
            rs_out.at[way, k, s, a], rs_in.at[way, k, s, a], "rs", (way, k, s, a), to
        )

    def rs_step(k, s, a):
        for way in range(2):
            if s == 0 and way != a:
                continue
            target = (z + NZ + (4 - s if way == 0 else s - 4)) % NZ
            term = part[k, a, chunk(target * CHUNK), :]
            for earlier in {2: (1, 0) if way == a else (1,), 3: (2,)}.get(s, ()):
                rs_copy(way, k, earlier, a).wait_recv()
                term = term + rs_in[way, k, earlier, a].astype(F32)
            rs_out[way, k, s, a] = term.astype(BF16)
            start(rs_copy(way, k, s, a))

    def y_exchange(k, a):
        return remote(y_out.at[k, a], y_in.at[k, a], "ye", (k, a), partner)

    def rs_end(k, a):
        for way in range(2):
            rs_copy(way, k, 3, a).wait_recv()
        y_out[k, a] = part[k, a, chunk(z * CHUNK), :] + (
            rs_in[0, k, 3, a].astype(F32) + rs_in[1, k, 3, a].astype(F32)
        )
        start(y_exchange(k, a))

    def ag_copy(way, k, s, a, origin):
        ref = ah.at[core, a, chunk(k * BLOCK + origin * CHUNK), :]
        to = z_over[way] if s == 3 else z_next[way]
        return remote(ref, ref, "ag", (way, k, s, a), to)

    def ag_origin(way, s):
        return (z + NZ + (-s if way == 0 else s)) % NZ

    def ag_step(k, s, a):
        for way in range(2):
            if s > 0:
                ag_copy(way, k, s - 1, a, ag_origin(way, s)).wait_recv()
            start(ag_copy(way, k, s, a, ag_origin(way, s)))
            if s == 2 and way == a:
                start(ag_copy(way, k, 3, a, ag_origin(way, 2)))

    def gelu(k):
        for a in range(2):
            y_exchange(k, a).wait_recv()
        value, grad = activate(y_out[k, 0] + y_in[k, 0], y_out[k, 1] + y_in[k, 1])
        rows = chunk(k * BLOCK + z * CHUNK)
        ah[core, 1, rows, :] = grad
        ag_step(k, 0, 1)
        ah[core, 0, rows, :] = value
        ag_step(k, 0, 0)

    def half_swap(k, a, half):
        ref = ah.at[half, a, k * BLOCK : (k + 1) * BLOCK, :]
        return remote(ref, ref, "cf", (k, a), twin)

    def ag_end(k, a):
        for way in range(2):
            ag_copy(way, k, 2, a, ag_origin(way, 3)).wait_recv()
        ag_copy(a, k, 3, a, ag_origin(a, 4)).wait_recv()
        start(half_swap(k, a, core))

    def g_piece(dx, dy):
        return g_sent.at[DY.index(dy), dx * PIECE : (dx + 1) * PIECE]

    def gx_copy(dx, dy):
        return remote(g_piece(dx, dy), gx_in.at[dx - 1, dy], "gx", (dx - 1, dy), x_peer[dx])

    def grad_block(k):
        half_swap(k, 1, other).wait_recv()
        rows = slice(k * BLOCK, (k + 1) * BLOCK)
        g[k] = nt(ah[0, 1, rows, :], w_full[:, 0:HALF]) + nt(
            ah[1, 1, rows, :], w_full[:, HALF:HIDDEN]
        )
        g_sent[k] = g[k].astype(BF16)
        for dx in (2, 1, 3):
            start(gx_copy(dx, DY[k]))

    def x_sum(dy):
        total = g[DY.index(dy), 0:PIECE]
        for dx in range(1, NX):
            gx_copy(dx, dy).wait_recv()
            total = total + gx_in[dx - 1, dy].astype(F32)
        return total

    def gy_copy(dy):
        if dy == 2:
            return remote(gy_far.at[0], gy_far.at[1], "gy", (dy - 1,), y_peer[dy])
        return remote(gy_out.at[dy - 1], gy_in.at[dy - 1], "gy", (dy - 1,), y_peer[dy])

    def y_part(dy):
        total = x_sum(dy)
        if dy == 2:
            gy_far[0] = total.astype(BF16)
        else:
            gy_out[dy - 1] = total
        start(gy_copy(dy))

    def weight_grads(a):
        for half in range(2):
            cols = slice(half * HALF, (half + 1) * HALF)
            if a == 1:
                grad_w_in[:, cols] = tn(panel[0, :, 0:WIDTH], ah[half, 1]).astype(BF16)
                continue
            if half == 0:
                for k in range(4):
                    half_swap(k, 0, other).wait_recv()
            grad_w_out[cols, :] = tn(ah[half, 0], panel[1, :, 0:WIDTH]).astype(BF16)

    for a in range(2):
        own[a].wait()
        for d in (1, 3):
            start(y_copy(d, a))
        own_ready(0, a)
    own[4].wait()
    own[5].wait()
    w_swap = [
        remote(w_full.at[:, other_cols], wi.at[WIDTH : 2 * WIDTH, :], "wx", (0,), twin),
        remote(wo_other, wo.at[:, WIDTH : 2 * WIDTH], "wx", (1,), twin),
    ]
    for copy in w_swap:
        start(copy)
    own[2].wait()
    own[3].wait()
    y_arrive(3, 0)
    x_arrive(0, 0)
    y_arrive(1, 0)
    x_arrive(0, 1)
    y_arrive(1, 1)
    for copy in w_swap:
        copy.wait_recv()
    matmuls(0, 0)
    rs_step(0, 0, 0)
    rs_step(0, 1, 0)
    y_arrive(3, 1)
    matmuls(0, 1)
    rs_step(0, 0, 1)
    rs_step(0, 1, 1)
    x_arrive(1, 0)
    y_arrive(2, 0)
    x_arrive(3, 0)
    matmuls(1, 0)
    rs_step(1, 0, 0)
    rs_step(1, 1, 0)
    rs_step(0, 2, 0)
    y_arrive(2, 1)
    x_arrive(3, 1)
    matmuls(2, 0)
    rs_step(2, 0, 0)
    rs_step(2, 1, 0)
    rs_step(0, 2, 1)
    x_arrive(1, 1)
    matmuls(2, 1)
    rs_step(2, 0, 1)
    rs_step(2, 1, 1)
    matmuls(1, 1)
    rs_step(1, 0, 1)
    rs_step(1, 1, 1)
    x_arrive(2, 0)
    matmuls(3, 0)
    rs_step(0, 3, 0)
    rs_step(3, 0, 0)
    rs_step(1, 2, 0)
    rs_step(3, 1, 0)
    x_arrive(2, 1)
    matmuls(3, 1)
    rs_step(0, 3, 1)
    rs_step(2, 2, 0)
    rs_step(3, 0, 1)
    rs_step(2, 2, 1)
    rs_step(3, 1, 1)
    rs_step(1, 2, 1)
    rs_end(0, 0)
    rs_step(1, 3, 0)
    rs_step(3, 2, 0)
    rs_end(0, 1)
    rs_step(2, 3, 0)
    rs_step(2, 3, 1)
    rs_step(3, 2, 1)
    rs_step(1, 3, 1)
    rs_end(1, 0)
    rs_step(3, 3, 0)
    gelu(0)
    rs_end(2, 0)
    rs_end(2, 1)
    rs_step(3, 3, 1)
    rs_end(1, 1)
    rs_end(3, 0)
    ag_step(0, 1, 1)
    ag_step(0, 1, 0)
    rs_end(3, 1)
    gelu(2)
    gelu(1)
    ag_step(0, 2, 1)
    ag_step(0, 2, 0)
    ag_step(2, 1, 1)
    gelu(3)
    ag_step(2, 1, 0)
    ag_step(1, 1, 1)
    ag_step(1, 1, 0)
    ag_end(0, 1)
    ag_step(2, 2, 1)
    ag_end(0, 0)
    ag_step(3, 1, 1)
    grad_block(0)
    ag_step(3, 1, 0)
    ag_step(2, 2, 0)
    ag_step(1, 2, 1)
    ag_step(1, 2, 0)
    ag_step(3, 2, 1)
    ag_end(2, 1)
    ag_step(3, 2, 0)
    grad_block(2)
    ag_end(2, 0)
    ag_end(1, 1)
    ag_end(1, 0)
    grad_block(1)
    ag_end(3, 1)
    y_part(3)
    ag_end(3, 0)
    grad_block(3)
    weight_grads(1)
    weight_grads(0)
    y_part(1)
    y_part(2)
    total = x_sum(0)
    for dy in range(1, NYH):
        gy_copy(dy).wait_recv()
        total = total + (gy_far[1].astype(F32) if dy == 2 else gy_in[dy - 1])
    grad_inputs[...] = total.astype(BF16)

    for copy in sent:
        copy.wait_send()


def store(*refs):
    half = len(refs) // 2
    sems = refs[-1]
    copies = [
        pltpu.make_async_copy(refs[i], refs[half + i], sems.at[i]) for i in range(half)
    ]
    for copy in copies:
        copy.start()
    for copy in copies:
        copy.wait()


def body(inputs, out_grad, w_in, w_out):
    hbm = pl.BlockSpec(memory_space=pltpu.HBM)
    vmem = pl.BlockSpec(memory_space=pltpu.VMEM)
    dma = pltpu.SemaphoreType.DMA
    shapes = ((PIECE, WIDTH), (WIDTH, HIDDEN), (HIDDEN, WIDTH))
    results = pl.pallas_call(
        kernel,
        out_shape=tuple(pltpu.VMEM(shape, BF16) for shape in shapes),
        in_specs=[hbm] * 4,
        out_specs=(vmem,) * 3,
        scratch_shapes=[
            pltpu.VMEM((2, TOKENS, 2 * WIDTH), BF16),
            pltpu.VMEM((2 * WIDTH, HALF), BF16),
            pltpu.VMEM((HALF, 2 * WIDTH), BF16),
            pltpu.VMEM((WIDTH, HIDDEN), BF16),
            pltpu.VMEM((HALF, WIDTH), BF16),
            pltpu.VMEM((4, 2, BLOCK, HALF), F32),
            pltpu.VMEM((2, 4, 4, 2, CHUNK, HALF), BF16),
            pltpu.VMEM((2, 4, 4, 2, CHUNK, HALF), BF16),
            pltpu.VMEM((4, 2, CHUNK, HALF), F32),
            pltpu.VMEM((4, 2, CHUNK, HALF), F32),
            pltpu.VMEM((2, 2, TOKENS, HALF), BF16),
            pltpu.VMEM((4, BLOCK, WIDTH), F32),
            pltpu.VMEM((3, 4, PIECE, WIDTH), BF16),
            pltpu.VMEM((3, PIECE, WIDTH), F32),
            pltpu.VMEM((3, PIECE, WIDTH), F32),
            pltpu.VMEM((4, BLOCK, WIDTH), BF16),
            pltpu.VMEM((2, PIECE, WIDTH), BF16),
            dma((6,)),
            *(dma(shape) for shape in SEMAPHORES.values() for _ in range(2)),
        ],
        compiler_params=pltpu.CompilerParams(
            collective_id=0, has_side_effects=True, vmem_limit_bytes=60 << 20
        ),
        cost_estimate=pl.CostEstimate(
            flops=6 * 10**9, bytes_accessed=5 * 10**6, transcendentals=10**6
        ),
        name="ffn_backward",
    )(inputs, out_grad, w_in, w_out)
    return pl.pallas_call(
        store,
        out_shape=tuple(jax.ShapeDtypeStruct(shape, BF16) for shape in shapes),
        in_specs=[pl.BlockSpec(memory_space=pl.ANY)] * 3,
        out_specs=(pl.BlockSpec(memory_space=pl.ANY),) * 3,
        scratch_shapes=[dma((3,))],
        compiler_params=pltpu.CompilerParams(vmem_limit_bytes=1 << 20),
        name="store_results",
    )(*results)


def solution(mesh):
    return jax.shard_map(
        body,
        mesh=mesh,
        in_specs=(P("col", "row"), P("col", "row"), P("row", "col"), P("col", "row")),
        out_specs=(P("col", "row"), P("row", "col"), P("col", "row")),
        check_vma=False,
    )
```

```python
import functools

import jax
import jax.numpy as jnp
from jax import lax
from jax.experimental import pallas as pl
from jax.experimental.pallas import tpu as pltpu
from jax.sharding import PartitionSpec as P

MESH = pl.DeviceIdType.MESH
BF16 = jnp.bfloat16
F32 = jnp.float32

slope_const = 0.7978845608028654
cubic_coef = 0.044715

NX, NYH, NYL, NZ = 4, 4, 2, 8
TOKENS = 512
BLOCK = TOKENS // 4
PIECE = TOKENS // (NX * NYH)
CHUNK = BLOCK // NZ
WIDTH = 384
HIDDEN = 1536
HALF = HIDDEN // 2
SUB = HALF // 2

DY = (0, 1, 3, 2)

SEMAPHORES = {
    "core": (2, 4, 4),
    "wx": (2,),
    "ys": (2, 2),
    "yf": (2,),
    "xs": (2, 3, 4),
    "rs": (2, 4, 3, 2),
    "rl": (2, 2, 4, 2),
    "rp": (4, 2),
    "ag": (2, 4, 4, 2),
    "ac": (2, 4, 2),
    "ap": (4, 2),
    "cf": (4, 2),
    "gx": (3, 4),
    "gy": (3,),
}


def nt(left, right):
    return lax.dot_general(
        left, right, (((1,), (1,)), ((), ())), preferred_element_type=F32
    )


def tn(left, right):
    return lax.dot_general(
        left, right, (((0,), (0,)), ((), ())), preferred_element_type=F32
    )


def activate(preact, upstream):
    square = preact * preact
    inner = slope_const * (preact + cubic_coef * square * preact)
    tanh_val = jnp.tanh(inner)
    deriv = slope_const * (1.0 + 3.0 * cubic_coef * square)
    value = 0.5 * preact * (1.0 + tanh_val)
    slope = 0.5 * (1.0 + tanh_val) + 0.5 * preact * (1.0 - tanh_val * tanh_val) * deriv
    return value.astype(BF16), (upstream * slope).astype(BF16)


def kernel(
    inputs, out_grad, w_in, w_out,
    grad_inputs, grad_w_in, grad_w_out,
    panel, wi, wo, w_full, wo_other, part, rs_out, rs_in, rs_last, rp_out, rp_in, ah,
    g, gx_in, gy_out, gy_in, g_sent, gy_far, local_sem, *pairs,
):
    row, col = lax.axis_index("row"), lax.axis_index("col")
    y_lo, z, core = row // 16, (row // 2) % 8, row % 2
    x, y_hi = col // 4, col % 4
    other = 1 - core

    def device(y_lo=y_lo, z=z, core=core, x=x, y_hi=y_hi):
        return ((y_lo * NZ + z) * 2 + core, x * NYH + y_hi)

    twin = device(core=other)
    partner = device(y_lo=1 - y_lo)
    z_next = (device(z=(z + 1) % NZ), device(z=(z + NZ - 1) % NZ))
    z_cross = tuple(device(z=(z + d) % NZ, y_lo=1 - y_lo) for d in (1, NZ - 1))
    z_over = (device(z=(z + 2) % NZ), device(z=(z + NZ - 2) % NZ))
    x_peer = [None, *(device(x=(x + d) % NX) for d in range(1, NX))]
    y_peer = [None, *(device(y_hi=(y_hi + d) % NYH) for d in range(1, NYH))]

    sems = {kind: pairs[2 * i : 2 * i + 2] for i, kind in enumerate(SEMAPHORES)}
    sent = []

    def remote(src, dst, kind, index, to):
        send, recv = sems[kind]
        return pltpu.make_async_remote_copy(
            src_ref=src, dst_ref=dst, send_sem=send.at[index], recv_sem=recv.at[index],
            device_id=to, device_id_type=MESH,
        )

    def start(copy):
        copy.start()
        sent.append(copy)

    half_cols = pl.ds(pl.multiple_of(core * HALF, 128), HALF)
    sub = pl.ds(pl.multiple_of(y_lo * SUB, 128), SUB)
    other_sub = pl.ds(pl.multiple_of((1 - y_lo) * SUB, 128), SUB)
    other_cols = pl.ds(pl.multiple_of(other * HALF, 128), HALF)
    own = [
        pltpu.make_async_copy(inputs, panel.at[0, 0:PIECE, 0:WIDTH], local_sem.at[0]),
        pltpu.make_async_copy(out_grad, panel.at[1, 0:PIECE, 0:WIDTH], local_sem.at[1]),
        pltpu.make_async_copy(w_in.at[:, half_cols], wi.at[0:WIDTH, :], local_sem.at[2]),
        pltpu.make_async_copy(w_out.at[half_cols, :], wo.at[:, 0:WIDTH], local_sem.at[3]),
        pltpu.make_async_copy(w_in, w_full, local_sem.at[4]),
        pltpu.make_async_copy(w_out.at[other_cols, :], wo_other, local_sem.at[5]),
    ]
    for copy in own:
        copy.start()

    barrier = pltpu.get_barrier_semaphore()
    greeted = [twin, partner, *z_next, *z_cross, *z_over, *x_peer[1:], *y_peer[1:]]
    for peer in greeted:
        pl.semaphore_signal(barrier, inc=1, device_id=peer, device_id_type=MESH)
    pl.semaphore_wait(barrier, len(greeted))

    def piece_rows(dx, dy):
        slot = 4 * DY.index(dy) + dx
        return slice(slot * PIECE, (slot + 1) * PIECE)

    def piece(dx, dy, a):
        return panel.at[a, piece_rows(dx, dy), 0:WIDTH]

    def to_twin(dx, dy, a):
        there = panel.at[a, piece_rows(dx, dy), WIDTH : 2 * WIDTH]
        return remote(piece(dx, dy, a), there, "core", (a, dx, dy), twin)

    def y_copy(d, a):
        return remote(piece(0, 0, a), piece(0, NYH - d, a), "ys", (a, d // 2), y_peer[d])

    def y_forward(a):
        d = 1 if a == 0 else 3
        return remote(piece(0, NYH - d, a), piece(0, 2, a), "yf", (a,), y_peer[d])

    def x_copy(d, dy, a):
        return remote(piece(0, dy, a), piece(NX - d, dy, a), "xs", (a, d - 1, dy), x_peer[d])

    def own_ready(dy, a):
        for d in (1, 3, 2):
            start(x_copy(d, dy, a))
        start(to_twin(0, dy, a))

    def y_arrive(d, a):
        if d == 2:
            y_forward(a).wait_recv()
        else:
            y_copy(d, a).wait_recv()
            if d == (1 if a == 0 else 3):
                start(y_forward(a))
        own_ready(NYH - d, a)

    def x_arrive(dy, a):
        for d in (1, 3, 2):
            x_copy(d, dy, a).wait_recv()
            start(to_twin(NX - d, dy, a))

    def matmuls(k, a):
        for dx in range(NX):
            to_twin(dx, DY[k], a).wait_recv()
        rows = slice(k * BLOCK, (k + 1) * BLOCK)
        if a == 0:
            part[k, 0] = jnp.dot(panel[0, rows, :], wi[...], preferred_element_type=F32)
        else:
            part[k, 1] = nt(panel[1, rows, :], wo[...])

    def chunk(start):
        return pl.ds(pl.multiple_of(start, 16), CHUNK)

    def rs_copy(way, k, s, a):
        to = z_over[way] if s == 0 else z_next[way]
        return remote(
            rs_out.at[way, k, s, a], rs_in.at[way, k, s, a], "rs", (way, k, s, a), to
        )

    def rl_copy(way, cross, k, a):
        return remote(
            rs_out.at[way, k, 3, a, :, other_sub if cross else sub],
            rs_last.at[way, cross, k, a], "rl", (way, cross, k, a),
            z_cross[way] if cross else z_next[way],
        )

    def rp_copy(k, a):
        return remote(rp_out.at[k, a], rp_in.at[k, a], "rp", (k, a), partner)

    def rs_step(k, s, a):
        for way in range(2):
            if s == 0 and way != a:
                continue
            target = (z + NZ + (4 - s if way == 0 else s - 4)) % NZ
            term = part[k, a, chunk(target * CHUNK), :]
            for earlier in {2: (1, 0) if way == a else (1,), 3: (2,)}.get(s, ()):
                rs_copy(way, k, earlier, a).wait_recv()
                term = term + rs_in[way, k, earlier, a].astype(F32)
            rs_out[way, k, s, a] = term.astype(BF16)
            if s < 3:
                start(rs_copy(way, k, s, a))
            else:
                start(rl_copy(way, 1, k, a))
                start(rl_copy(way, 0, k, a))
        if s == 0:
            rp_out[k, a] = part[k, a, chunk(z * CHUNK), other_sub].astype(BF16)
            start(rp_copy(k, a))

    def ag_copy(way, k, s, a, origin):
        rows = chunk(k * BLOCK + origin * CHUNK)
        ref = ah.at[core, a, rows, sub] if s == 0 else ah.at[core, a, rows, :]
        to = z_over[way] if s == 3 else z_next[way]
        return remote(ref, ref, "ag", (way, k, s, a), to)

    def ag_cross(way, k, a, origin, cols):
        ref = ah.at[core, a, chunk(k * BLOCK + origin * CHUNK), cols]
        return remote(ref, ref, "ac", (way, k, a), z_cross[way])

    def ag_partner(k, a, cols):
        ref = ah.at[core, a, chunk(k * BLOCK + z * CHUNK), cols]
        return remote(ref, ref, "ap", (k, a), partner)

    def ag_origin(way, s):
        return (z + NZ + (-s if way == 0 else s)) % NZ

    def ag_step(k, s, a):
        for way in range(2):
            origin = ag_origin(way, s)
            if s == 0:
                start(ag_cross(way, k, a, origin, sub))
            else:
                ag_copy(way, k, s - 1, a, origin).wait_recv()
            if s == 1:
                ag_cross(way, k, a, origin, other_sub).wait_recv()
            start(ag_copy(way, k, s, a, origin))
            if s == 2 and way == a:
                start(ag_copy(way, k, 3, a, origin))
        if s == 0:
            start(ag_partner(k, a, sub))

    def gelu(k):
        sums = []
        for a in range(2):
            rp_copy(k, a).wait_recv()
            total = part[k, a, chunk(z * CHUNK), sub] + rp_in[k, a].astype(F32)
            for way in range(2):
                for cross in range(2):
                    rl_copy(way, cross, k, a).wait_recv()
                    total = total + rs_last[way, cross, k, a].astype(F32)
            sums.append(total)
        value, grad = activate(*sums)
        rows = chunk(k * BLOCK + z * CHUNK)
        ah[core, 1, rows, sub] = grad
        ag_step(k, 0, 1)
        ah[core, 0, rows, sub] = value
        ag_step(k, 0, 0)

    def half_swap(k, a, half):
        ref = ah.at[half, a, k * BLOCK : (k + 1) * BLOCK, :]
        return remote(ref, ref, "cf", (k, a), twin)

    def ag_end(k, a):
        for way in range(2):
            ag_copy(way, k, 2, a, ag_origin(way, 3)).wait_recv()
        ag_copy(a, k, 3, a, ag_origin(a, 4)).wait_recv()
        ag_partner(k, a, other_sub).wait_recv()
        start(half_swap(k, a, core))

    def g_piece(dx, dy):
        return g_sent.at[DY.index(dy), dx * PIECE : (dx + 1) * PIECE]

    def gx_copy(dx, dy):
        return remote(g_piece(dx, dy), gx_in.at[dx - 1, dy], "gx", (dx - 1, dy), x_peer[dx])

    def grad_block(k):
        half_swap(k, 1, other).wait_recv()
        rows = slice(k * BLOCK, (k + 1) * BLOCK)
        g[k] = nt(ah[0, 1, rows, :], w_full[:, 0:HALF]) + nt(
            ah[1, 1, rows, :], w_full[:, HALF:HIDDEN]
        )
        g_sent[k] = g[k].astype(BF16)
        for dx in (2, 1, 3):
            start(gx_copy(dx, DY[k]))

    def x_sum(dy):
        total = g[DY.index(dy), 0:PIECE]
        for dx in range(1, NX):
            gx_copy(dx, dy).wait_recv()
            total = total + gx_in[dx - 1, dy].astype(F32)
        return total

    def gy_copy(dy):
        if dy == 2:
            return remote(gy_far.at[0], gy_far.at[1], "gy", (dy - 1,), y_peer[dy])
        return remote(gy_out.at[dy - 1], gy_in.at[dy - 1], "gy", (dy - 1,), y_peer[dy])

    def y_part(dy):
        total = x_sum(dy)
        if dy == 2:
            gy_far[0] = total.astype(BF16)
        else:
            gy_out[dy - 1] = total
        start(gy_copy(dy))

    def weight_grads(a):
        for half in range(2):
            cols = slice(half * HALF, (half + 1) * HALF)
            if a == 1:
                grad_w_in[:, cols] = tn(panel[0, :, 0:WIDTH], ah[half, 1]).astype(BF16)
                continue
            if half == 0:
                for k in range(4):
                    half_swap(k, 0, other).wait_recv()
            grad_w_out[cols, :] = tn(ah[half, 0], panel[1, :, 0:WIDTH]).astype(BF16)

    for a in range(2):
        own[a].wait()
        for d in (1, 3):
            start(y_copy(d, a))
        own_ready(0, a)
    own[4].wait()
    own[5].wait()
    w_swap = [
        remote(w_full.at[:, other_cols], wi.at[WIDTH : 2 * WIDTH, :], "wx", (0,), twin),
        remote(wo_other, wo.at[:, WIDTH : 2 * WIDTH], "wx", (1,), twin),
    ]
    for copy in w_swap:
        start(copy)
    own[2].wait()
    own[3].wait()
    y_arrive(1, 0)
    y_arrive(3, 0)
    x_arrive(0, 0)
    y_arrive(1, 1)
    x_arrive(0, 1)
    y_arrive(3, 1)
    for copy in w_swap:
        copy.wait_recv()
    matmuls(0, 0)
    rs_step(0, 0, 0)
    rs_step(0, 1, 0)
    matmuls(0, 1)
    rs_step(0, 0, 1)
    rs_step(0, 1, 1)
    x_arrive(3, 0)
    y_arrive(2, 0)
    x_arrive(1, 0)
    matmuls(2, 0)
    rs_step(2, 0, 0)
    rs_step(2, 1, 0)
    rs_step(0, 2, 0)
    y_arrive(2, 1)
    x_arrive(3, 1)
    matmuls(1, 0)
    rs_step(1, 0, 0)
    rs_step(1, 1, 0)
    rs_step(0, 2, 1)
    x_arrive(1, 1)
    matmuls(2, 1)
    rs_step(2, 0, 1)
    rs_step(2, 1, 1)
    matmuls(1, 1)
    rs_step(1, 0, 1)
    rs_step(1, 1, 1)
    x_arrive(2, 0)
    rs_step(2, 2, 0)
    matmuls(3, 0)
    rs_step(0, 3, 0)
    rs_step(3, 0, 0)
    rs_step(3, 1, 0)
    x_arrive(2, 1)
    rs_step(1, 2, 0)
    matmuls(3, 1)
    rs_step(3, 0, 1)
    rs_step(3, 1, 1)
    rs_step(2, 2, 1)
    rs_step(0, 3, 1)
    rs_step(1, 2, 1)
    rs_step(2, 3, 0)
    rs_step(3, 2, 0)
    rs_step(1, 3, 0)
    rs_step(3, 2, 1)
    rs_step(2, 3, 1)
    gelu(0)
    rs_step(1, 3, 1)
    rs_step(3, 3, 0)
    rs_step(3, 3, 1)
    gelu(2)
    ag_step(0, 1, 1)
    ag_step(0, 1, 0)
    gelu(1)
    gelu(3)
    ag_step(2, 1, 1)
    ag_step(0, 2, 1)
    ag_step(2, 1, 0)
    ag_step(0, 2, 0)
    ag_step(1, 1, 1)
    ag_step(1, 1, 0)
    ag_step(2, 2, 1)
    ag_step(3, 1, 1)
    ag_step(3, 1, 0)
    ag_step(2, 2, 0)
    ag_end(0, 1)
    ag_step(1, 2, 1)
    ag_end(0, 0)
    grad_block(0)
    ag_step(1, 2, 0)
    ag_step(3, 2, 1)
    ag_end(2, 1)
    ag_step(3, 2, 0)
    grad_block(2)
    ag_end(2, 0)
    ag_end(1, 1)
    ag_end(1, 0)
    grad_block(1)
    ag_end(3, 1)
    ag_end(3, 0)
    y_part(3)
    grad_block(3)
    weight_grads(1)
    weight_grads(0)
    y_part(1)
    y_part(2)
    total = x_sum(0)
    for dy in range(1, NYH):
        gy_copy(dy).wait_recv()
        total = total + (gy_far[1].astype(F32) if dy == 2 else gy_in[dy - 1])
    grad_inputs[...] = total.astype(BF16)

    for copy in sent:
        copy.wait_send()


def store(*refs):
    half = len(refs) // 2
    sems = refs[-1]
    copies = [
        pltpu.make_async_copy(refs[i], refs[half + i], sems.at[i]) for i in range(half)
    ]
    for copy in copies:
        copy.start()
    for copy in copies:
        copy.wait()


def body(inputs, out_grad, w_in, w_out):
    hbm = pl.BlockSpec(memory_space=pltpu.HBM)
    vmem = pl.BlockSpec(memory_space=pltpu.VMEM)
    dma = pltpu.SemaphoreType.DMA
    shapes = ((PIECE, WIDTH), (WIDTH, HIDDEN), (HIDDEN, WIDTH))
    results = pl.pallas_call(
        kernel,
        out_shape=tuple(pltpu.VMEM(shape, BF16) for shape in shapes),
        in_specs=[hbm] * 4,
        out_specs=(vmem,) * 3,
        scratch_shapes=[
            pltpu.VMEM((2, TOKENS, 2 * WIDTH), BF16),
            pltpu.VMEM((2 * WIDTH, HALF), BF16),
            pltpu.VMEM((HALF, 2 * WIDTH), BF16),
            pltpu.VMEM((WIDTH, HIDDEN), BF16),
            pltpu.VMEM((HALF, WIDTH), BF16),
            pltpu.VMEM((4, 2, BLOCK, HALF), F32),
            pltpu.VMEM((2, 4, 4, 2, CHUNK, HALF), BF16),
            pltpu.VMEM((2, 4, 4, 2, CHUNK, HALF), BF16),
            pltpu.VMEM((2, 2, 4, 2, CHUNK, SUB), BF16),
            pltpu.VMEM((4, 2, CHUNK, SUB), BF16),
            pltpu.VMEM((4, 2, CHUNK, SUB), BF16),
            pltpu.VMEM((2, 2, TOKENS, HALF), BF16),
            pltpu.VMEM((4, BLOCK, WIDTH), F32),
            pltpu.VMEM((3, 4, PIECE, WIDTH), BF16),
            pltpu.VMEM((3, PIECE, WIDTH), F32),
            pltpu.VMEM((3, PIECE, WIDTH), F32),
            pltpu.VMEM((4, BLOCK, WIDTH), BF16),
            pltpu.VMEM((2, PIECE, WIDTH), BF16),
            dma((6,)),
            *(dma(shape) for shape in SEMAPHORES.values() for _ in range(2)),
        ],
        compiler_params=pltpu.CompilerParams(
            collective_id=0, has_side_effects=True, vmem_limit_bytes=60 << 20
        ),
        cost_estimate=pl.CostEstimate(
            flops=6 * 10**9, bytes_accessed=5 * 10**6, transcendentals=10**6
        ),
        name="ffn_backward",
    )(inputs, out_grad, w_in, w_out)
    return pl.pallas_call(
        store,
        out_shape=tuple(jax.ShapeDtypeStruct(shape, BF16) for shape in shapes),
        in_specs=[pl.BlockSpec(memory_space=pl.ANY)] * 3,
        out_specs=(pl.BlockSpec(memory_space=pl.ANY),) * 3,
        scratch_shapes=[dma((3,))],
        compiler_params=pltpu.CompilerParams(vmem_limit_bytes=1 << 20),
        name="store_results",
    )(*results)


def solution(mesh):
    return jax.shard_map(
        body,
        mesh=mesh,
        in_specs=(P("col", "row"), P("col", "row"), P("row", "col"), P("col", "row")),
        out_specs=(P("col", "row"), P("row", "col"), P("col", "row")),
        check_vma=False,
    )
```

```python
import functools

import jax
import jax.numpy as jnp
from jax import lax
from jax.experimental import pallas as pl
from jax.experimental.pallas import tpu as pltpu
from jax.sharding import PartitionSpec as P

MESH = pl.DeviceIdType.MESH
BF16 = jnp.bfloat16
F32 = jnp.float32

slope_const = 0.7978845608028654
cubic_coef = 0.044715

NX, NYH, NYL, NZ = 4, 4, 2, 8
TOKENS = 512
BLOCK = TOKENS // 4
PIECE = TOKENS // (NX * NYH)
CHUNK = BLOCK // NZ
WIDTH = 384
HIDDEN = 1536
HALF = HIDDEN // 2
SUB = HALF // 2

DY = (0, 1, 3, 2)

SEMAPHORES = {
    "core": (2, 4, 4),
    "wx": (2,),
    "ys": (2, 2),
    "yf": (2,),
    "xs": (2, 3, 4),
    "rs": (2, 4, 3, 2),
    "rl": (2, 2, 4, 2),
    "rp": (4, 2),
    "ag": (2, 4, 4, 2),
    "ac": (2, 4),
    "ap": (4,),
    "aq": (4,),
    "cf": (4, 2),
    "gx": (3, 4),
    "gy": (3,),
}


def nt(left, right):
    return lax.dot_general(
        left, right, (((1,), (1,)), ((), ())), preferred_element_type=F32
    )


def tn(left, right):
    return lax.dot_general(
        left, right, (((0,), (0,)), ((), ())), preferred_element_type=F32
    )


def activate(preact, upstream):
    square = preact * preact
    inner = slope_const * (preact + cubic_coef * square * preact)
    tanh_val = jnp.tanh(inner)
    deriv = slope_const * (1.0 + 3.0 * cubic_coef * square)
    value = 0.5 * preact * (1.0 + tanh_val)
    slope = 0.5 * (1.0 + tanh_val) + 0.5 * preact * (1.0 - tanh_val * tanh_val) * deriv
    return value.astype(BF16), (upstream * slope).astype(BF16)


def kernel(
    inputs, out_grad, w_in, w_out,
    grad_inputs, grad_w_in, grad_w_out,
    panel, wi, wo, w_full, wo_other, part, rs_out, rs_in, rs_last, rp_out, rp_in, ah,
    g, gx_in, gy_out, gy_in, g_sent, gy_far, local_sem, *pairs,
):
    row, col = lax.axis_index("row"), lax.axis_index("col")
    y_lo, z, core = row // 16, (row // 2) % 8, row % 2
    x, y_hi = col // 4, col % 4
    other = 1 - core

    def device(y_lo=y_lo, z=z, core=core, x=x, y_hi=y_hi):
        return ((y_lo * NZ + z) * 2 + core, x * NYH + y_hi)

    twin = device(core=other)
    partner = device(y_lo=1 - y_lo)
    z_next = (device(z=(z + 1) % NZ), device(z=(z + NZ - 1) % NZ))
    z_cross = tuple(device(z=(z + d) % NZ, y_lo=1 - y_lo) for d in (1, NZ - 1))
    z_over = (device(z=(z + 2) % NZ), device(z=(z + NZ - 2) % NZ))
    x_peer = [None, *(device(x=(x + d) % NX) for d in range(1, NX))]
    y_peer = [None, *(device(y_hi=(y_hi + d) % NYH) for d in range(1, NYH))]

    sems = {kind: pairs[2 * i : 2 * i + 2] for i, kind in enumerate(SEMAPHORES)}
    sent = []

    def remote(src, dst, kind, index, to):
        send, recv = sems[kind]
        return pltpu.make_async_remote_copy(
            src_ref=src, dst_ref=dst, send_sem=send.at[index], recv_sem=recv.at[index],
            device_id=to, device_id_type=MESH,
        )

    def start(copy):
        copy.start()
        sent.append(copy)

    half_cols = pl.ds(pl.multiple_of(core * HALF, 128), HALF)
    sub = pl.ds(pl.multiple_of(y_lo * SUB, 128), SUB)
    other_sub = pl.ds(pl.multiple_of((1 - y_lo) * SUB, 128), SUB)
    other_cols = pl.ds(pl.multiple_of(other * HALF, 128), HALF)
    own = [
        pltpu.make_async_copy(inputs, panel.at[0, 0:PIECE, 0:WIDTH], local_sem.at[0]),
        pltpu.make_async_copy(out_grad, panel.at[1, 0:PIECE, 0:WIDTH], local_sem.at[1]),
        pltpu.make_async_copy(w_in.at[:, half_cols], wi.at[0:WIDTH, :], local_sem.at[2]),
        pltpu.make_async_copy(w_out.at[half_cols, :], wo.at[:, 0:WIDTH], local_sem.at[3]),
        pltpu.make_async_copy(w_in, w_full, local_sem.at[4]),
        pltpu.make_async_copy(w_out.at[other_cols, :], wo_other, local_sem.at[5]),
    ]
    for copy in own:
        copy.start()

    barrier = pltpu.get_barrier_semaphore()
    greeted = [twin, partner, *z_next, *z_cross, *z_over, *x_peer[1:], *y_peer[1:]]
    for peer in greeted:
        pl.semaphore_signal(barrier, inc=1, device_id=peer, device_id_type=MESH)
    pl.semaphore_wait(barrier, len(greeted))

    def piece_rows(dx, dy):
        slot = 4 * DY.index(dy) + dx
        return slice(slot * PIECE, (slot + 1) * PIECE)

    def piece(dx, dy, a):
        return panel.at[a, piece_rows(dx, dy), 0:WIDTH]

    def to_twin(dx, dy, a):
        there = panel.at[a, piece_rows(dx, dy), WIDTH : 2 * WIDTH]
        return remote(piece(dx, dy, a), there, "core", (a, dx, dy), twin)

    def y_copy(d, a):
        return remote(piece(0, 0, a), piece(0, NYH - d, a), "ys", (a, d // 2), y_peer[d])

    def y_forward(a):
        d = 1 if a == 0 else 3
        return remote(piece(0, NYH - d, a), piece(0, 2, a), "yf", (a,), y_peer[d])

    def x_copy(d, dy, a):
        return remote(piece(0, dy, a), piece(NX - d, dy, a), "xs", (a, d - 1, dy), x_peer[d])

    def own_ready(dy, a):
        for d in (1, 3, 2):
            start(x_copy(d, dy, a))
        start(to_twin(0, dy, a))

    def y_arrive(d, a):
        if d == 2:
            y_forward(a).wait_recv()
        else:
            y_copy(d, a).wait_recv()
            if d == (1 if a == 0 else 3):
                start(y_forward(a))
        own_ready(NYH - d, a)

    def x_arrive(dy, a):
        for d in (1, 3, 2):
            x_copy(d, dy, a).wait_recv()
            start(to_twin(NX - d, dy, a))

    def matmuls(k, a):
        for dx in range(NX):
            to_twin(dx, DY[k], a).wait_recv()
        rows = slice(k * BLOCK, (k + 1) * BLOCK)
        if a == 0:
            part[k, 0] = jnp.dot(panel[0, rows, :], wi[...], preferred_element_type=F32)
        else:
            part[k, 1] = nt(panel[1, rows, :], wo[...])

    def chunk(start):
        return pl.ds(pl.multiple_of(start, 16), CHUNK)

    def rs_copy(way, k, s, a):
        to = z_over[way] if s == 0 else z_next[way]
        return remote(
            rs_out.at[way, k, s, a], rs_in.at[way, k, s, a], "rs", (way, k, s, a), to
        )

    def rl_copy(way, cross, k, a):
        return remote(
            rs_out.at[way, k, 3, a, :, other_sub if cross else sub],
            rs_last.at[way, cross, k, a], "rl", (way, cross, k, a),
            z_cross[way] if cross else z_next[way],
        )

    def rp_copy(k, a):
        return remote(rp_out.at[k, a], rp_in.at[k, a], "rp", (k, a), partner)

    def rs_step(k, s, a):
        for way in range(2):
            if s == 0 and way != a:
                continue
            target = (z + NZ + (4 - s if way == 0 else s - 4)) % NZ
            term = part[k, a, chunk(target * CHUNK), :]
            for earlier in {2: (1, 0) if way == a else (1,), 3: (2,)}.get(s, ()):
                rs_copy(way, k, earlier, a).wait_recv()
                term = term + rs_in[way, k, earlier, a].astype(F32)
            rs_out[way, k, s, a] = term.astype(BF16)
            if s < 3:
                start(rs_copy(way, k, s, a))
            else:
                start(rl_copy(way, 1, k, a))
                start(rl_copy(way, 0, k, a))
        if s == 0:
            rp_out[k, a] = part[k, a, chunk(z * CHUNK), other_sub].astype(BF16)
            start(rp_copy(k, a))

    def ag_copy(way, k, s, a, origin):
        rows = chunk(k * BLOCK + origin * CHUNK)
        ref = ah.at[core, a, rows, sub] if s == 0 or a == 0 else ah.at[core, a, rows, :]
        to = z_over[way] if s == 3 else z_next[way]
        return remote(ref, ref, "ag", (way, k, s, a), to)

    def ag_cross(way, k, origin, cols):
        ref = ah.at[core, 1, chunk(k * BLOCK + origin * CHUNK), cols]
        return remote(ref, ref, "ac", (way, k), z_cross[way])

    def ag_partner(k, cols):
        ref = ah.at[core, 1, chunk(k * BLOCK + z * CHUNK), cols]
        return remote(ref, ref, "ap", (k,), partner)

    def act_swap(k, cols):
        ref = ah.at[core, 0, k * BLOCK : (k + 1) * BLOCK, cols]
        return remote(ref, ref, "aq", (k,), partner)

    def ag_origin(way, s):
        return (z + NZ + (-s if way == 0 else s)) % NZ

    def ag_step(k, s, a):
        for way in range(2):
            origin = ag_origin(way, s)
            if s == 0 and a == 1:
                start(ag_cross(way, k, origin, sub))
            if s > 0:
                ag_copy(way, k, s - 1, a, origin).wait_recv()
            if s == 1 and a == 1:
                ag_cross(way, k, origin, other_sub).wait_recv()
            start(ag_copy(way, k, s, a, origin))
            if s == 2 and way == a:
                start(ag_copy(way, k, 3, a, origin))
        if s == 0 and a == 1:
            start(ag_partner(k, sub))

    def gelu(k):
        sums = []
        for a in range(2):
            rp_copy(k, a).wait_recv()
            total = part[k, a, chunk(z * CHUNK), sub] + rp_in[k, a].astype(F32)
            for way in range(2):
                for cross in range(2):
                    rl_copy(way, cross, k, a).wait_recv()
                    total = total + rs_last[way, cross, k, a].astype(F32)
            sums.append(total)
        value, grad = activate(*sums)
        rows = chunk(k * BLOCK + z * CHUNK)
        ah[core, 1, rows, sub] = grad
        ag_step(k, 0, 1)
        ah[core, 0, rows, sub] = value
        ag_step(k, 0, 0)

    def half_swap(k, a, half):
        ref = ah.at[half, a, k * BLOCK : (k + 1) * BLOCK, :]
        return remote(ref, ref, "cf", (k, a), twin)

    def ag_end(k, a):
        for way in range(2):
            ag_copy(way, k, 2, a, ag_origin(way, 3)).wait_recv()
        ag_copy(a, k, 3, a, ag_origin(a, 4)).wait_recv()
        if a == 0:
            start(act_swap(k, sub))
        else:
            ag_partner(k, other_sub).wait_recv()
            start(half_swap(k, 1, core))

    def act_end(k):
        act_swap(k, other_sub).wait_recv()
        start(half_swap(k, 0, core))

    def g_piece(dx, dy):
        return g_sent.at[DY.index(dy), dx * PIECE : (dx + 1) * PIECE]

    def gx_copy(dx, dy):
        return remote(g_piece(dx, dy), gx_in.at[dx - 1, dy], "gx", (dx - 1, dy), x_peer[dx])

    def grad_block(k):
        half_swap(k, 1, other).wait_recv()
        rows = slice(k * BLOCK, (k + 1) * BLOCK)
        g[k] = nt(ah[0, 1, rows, :], w_full[:, 0:HALF]) + nt(
            ah[1, 1, rows, :], w_full[:, HALF:HIDDEN]
        )
        g_sent[k] = g[k].astype(BF16)
        for dx in (2, 1, 3):
            start(gx_copy(dx, DY[k]))

    def x_sum(dy):
        total = g[DY.index(dy), 0:PIECE]
        for dx in range(1, NX):
            gx_copy(dx, dy).wait_recv()
            total = total + gx_in[dx - 1, dy].astype(F32)
        return total

    def gy_copy(dy):
        if dy == 2:
            return remote(gy_far.at[0], gy_far.at[1], "gy", (dy - 1,), y_peer[dy])
        return remote(gy_out.at[dy - 1], gy_in.at[dy - 1], "gy", (dy - 1,), y_peer[dy])

    def y_part(dy):
        total = x_sum(dy)
        if dy == 2:
            gy_far[0] = total.astype(BF16)
        else:
            gy_out[dy - 1] = total
        start(gy_copy(dy))

    def weight_grads(a):
        for half in range(2):
            cols = slice(half * HALF, (half + 1) * HALF)
            if a == 1:
                grad_w_in[:, cols] = tn(panel[0, :, 0:WIDTH], ah[half, 1]).astype(BF16)
                continue
            if half == 0:
                for k in range(4):
                    half_swap(k, 0, other).wait_recv()
            grad_w_out[cols, :] = tn(ah[half, 0], panel[1, :, 0:WIDTH]).astype(BF16)

    for a in range(2):
        own[a].wait()
        for d in (1, 3):
            start(y_copy(d, a))
        own_ready(0, a)
    own[4].wait()
    own[5].wait()
    w_swap = [
        remote(w_full.at[:, other_cols], wi.at[WIDTH : 2 * WIDTH, :], "wx", (0,), twin),
        remote(wo_other, wo.at[:, WIDTH : 2 * WIDTH], "wx", (1,), twin),
    ]
    for copy in w_swap:
        start(copy)
    own[2].wait()
    own[3].wait()
    y_arrive(3, 0)
    x_arrive(0, 0)
    y_arrive(1, 0)
    y_arrive(3, 1)
    y_arrive(1, 1)
    x_arrive(0, 1)
    for copy in w_swap:
        copy.wait_recv()
    matmuls(0, 0)
    rs_step(0, 0, 0)
    rs_step(0, 1, 0)
    matmuls(0, 1)
    rs_step(0, 0, 1)
    rs_step(0, 1, 1)
    x_arrive(1, 0)
    y_arrive(2, 0)
    x_arrive(3, 0)
    matmuls(1, 0)
    y_arrive(2, 1)
    rs_step(1, 0, 0)
    rs_step(0, 2, 0)
    rs_step(1, 1, 0)
    x_arrive(1, 1)
    matmuls(2, 0)
    rs_step(2, 0, 0)
    rs_step(2, 1, 0)
    x_arrive(3, 1)
    matmuls(1, 1)
    rs_step(1, 0, 1)
    rs_step(1, 1, 1)
    rs_step(0, 2, 1)
    matmuls(2, 1)
    rs_step(2, 0, 1)
    rs_step(2, 1, 1)
    x_arrive(2, 0)
    matmuls(3, 0)
    rs_step(3, 0, 0)
    rs_step(0, 3, 0)
    x_arrive(2, 1)
    rs_step(1, 2, 0)
    rs_step(3, 1, 0)
    matmuls(3, 1)
    rs_step(3, 0, 1)
    rs_step(3, 1, 1)
    rs_step(1, 2, 1)
    rs_step(2, 2, 0)
    rs_step(0, 3, 1)
    rs_step(2, 2, 1)
    rs_step(1, 3, 0)
    rs_step(3, 2, 0)
    rs_step(3, 2, 1)
    rs_step(1, 3, 1)
    rs_step(2, 3, 0)
    gelu(0)
    rs_step(2, 3, 1)
    rs_step(3, 3, 0)
    rs_step(3, 3, 1)
    gelu(1)
    ag_step(0, 1, 0)
    ag_step(0, 1, 1)
    gelu(2)
    gelu(3)
    ag_step(1, 1, 0)
    ag_step(1, 1, 1)
    ag_step(0, 2, 0)
    ag_step(0, 2, 1)
    ag_step(2, 1, 0)
    ag_step(2, 1, 1)
    ag_step(3, 1, 0)
    ag_step(1, 2, 0)
    ag_step(3, 1, 1)
    ag_step(1, 2, 1)
    ag_end(0, 0)
    ag_step(2, 2, 0)
    ag_end(0, 1)
    ag_step(2, 2, 1)
    ag_step(3, 2, 0)
    grad_block(0)
    ag_end(1, 0)
    ag_step(3, 2, 1)
    ag_end(1, 1)
    ag_end(2, 0)
    act_end(0)
    grad_block(1)
    ag_end(2, 1)
    ag_end(3, 0)
    grad_block(2)
    ag_end(3, 1)
    act_end(1)
    grad_block(3)
    weight_grads(1)
    y_part(1)
    act_end(2)
    act_end(3)
    y_part(3)
    weight_grads(0)
    y_part(2)
    total = x_sum(0)
    for dy in range(1, NYH):
        gy_copy(dy).wait_recv()
        total = total + (gy_far[1].astype(F32) if dy == 2 else gy_in[dy - 1])
    grad_inputs[...] = total.astype(BF16)

    for copy in sent:
        copy.wait_send()


def store(*refs):
    half = len(refs) // 2
    sems = refs[-1]
    copies = [
        pltpu.make_async_copy(refs[i], refs[half + i], sems.at[i]) for i in range(half)
    ]
    for copy in copies:
        copy.start()
    for copy in copies:
        copy.wait()


def body(inputs, out_grad, w_in, w_out):
    hbm = pl.BlockSpec(memory_space=pltpu.HBM)
    vmem = pl.BlockSpec(memory_space=pltpu.VMEM)
    dma = pltpu.SemaphoreType.DMA
    shapes = ((PIECE, WIDTH), (WIDTH, HIDDEN), (HIDDEN, WIDTH))
    results = pl.pallas_call(
        kernel,
        out_shape=tuple(pltpu.VMEM(shape, BF16) for shape in shapes),
        in_specs=[hbm] * 4,
        out_specs=(vmem,) * 3,
        scratch_shapes=[
            pltpu.VMEM((2, TOKENS, 2 * WIDTH), BF16),
            pltpu.VMEM((2 * WIDTH, HALF), BF16),
            pltpu.VMEM((HALF, 2 * WIDTH), BF16),
            pltpu.VMEM((WIDTH, HIDDEN), BF16),
            pltpu.VMEM((HALF, WIDTH), BF16),
            pltpu.VMEM((4, 2, BLOCK, HALF), F32),
            pltpu.VMEM((2, 4, 4, 2, CHUNK, HALF), BF16),
            pltpu.VMEM((2, 4, 4, 2, CHUNK, HALF), BF16),
            pltpu.VMEM((2, 2, 4, 2, CHUNK, SUB), BF16),
            pltpu.VMEM((4, 2, CHUNK, SUB), BF16),
            pltpu.VMEM((4, 2, CHUNK, SUB), BF16),
            pltpu.VMEM((2, 2, TOKENS, HALF), BF16),
            pltpu.VMEM((4, BLOCK, WIDTH), F32),
            pltpu.VMEM((3, 4, PIECE, WIDTH), BF16),
            pltpu.VMEM((3, PIECE, WIDTH), F32),
            pltpu.VMEM((3, PIECE, WIDTH), F32),
            pltpu.VMEM((4, BLOCK, WIDTH), BF16),
            pltpu.VMEM((2, PIECE, WIDTH), BF16),
            dma((6,)),
            *(dma(shape) for shape in SEMAPHORES.values() for _ in range(2)),
        ],
        compiler_params=pltpu.CompilerParams(
            collective_id=0, has_side_effects=True, vmem_limit_bytes=60 << 20
        ),
        cost_estimate=pl.CostEstimate(
            flops=6 * 10**9, bytes_accessed=5 * 10**6, transcendentals=10**6
        ),
        name="ffn_backward",
    )(inputs, out_grad, w_in, w_out)
    return pl.pallas_call(
        store,
        out_shape=tuple(jax.ShapeDtypeStruct(shape, BF16) for shape in shapes),
        in_specs=[pl.BlockSpec(memory_space=pl.ANY)] * 3,
        out_specs=(pl.BlockSpec(memory_space=pl.ANY),) * 3,
        scratch_shapes=[dma((3,))],
        compiler_params=pltpu.CompilerParams(vmem_limit_bytes=1 << 20),
        name="store_results",
    )(*results)


def solution(mesh):
    return jax.shard_map(
        body,
        mesh=mesh,
        in_specs=(P("col", "row"), P("col", "row"), P("row", "col"), P("col", "row")),
        out_specs=(P("col", "row"), P("row", "col"), P("col", "row")),
        check_vma=False,
    )
```

```python
import functools

import jax
import jax.numpy as jnp
from jax import lax
from jax.experimental import pallas as pl
from jax.experimental.pallas import tpu as pltpu
from jax.sharding import PartitionSpec as P

MESH = pl.DeviceIdType.MESH
BF16 = jnp.bfloat16
F32 = jnp.float32

slope_const = 0.7978845608028654
cubic_coef = 0.044715

NX, NYH, NYL, NZ = 4, 4, 2, 8
TOKENS = 512
BLOCK = TOKENS // 4
PIECE = TOKENS // (NX * NYH)
CHUNK = BLOCK // NZ
WIDTH = 384
HIDDEN = 1536
HALF = HIDDEN // 2
SUB = HALF // 2

DY = (0, 1, 3, 2)

STORES = 4

SEMAPHORES = {
    "core": (2, 4, 4),
    "wx": (2,),
    "ys": (2, 2),
    "yf": (2,),
    "xs": (2, 3, 4),
    "rs": (2, 4, 3, 2),
    "rl": (2, 2, 4, 2),
    "rp": (4, 2),
    "ag": (2, 4, 4, 2),
    "ac": (2, 4),
    "ap": (4,),
    "aq": (4,),
    "cf": (4, 2),
    "gx": (3, 4),
    "gy": (3,),
}


def nt(left, right):
    return lax.dot_general(
        left, right, (((1,), (1,)), ((), ())), preferred_element_type=F32
    )


def tn(left, right):
    return lax.dot_general(
        left, right, (((0,), (0,)), ((), ())), preferred_element_type=F32
    )


def activate(preact, upstream):
    square = preact * preact
    inner = slope_const * (preact + cubic_coef * square * preact)
    tanh_val = jnp.tanh(inner)
    deriv = slope_const * (1.0 + 3.0 * cubic_coef * square)
    value = 0.5 * preact * (1.0 + tanh_val)
    slope = 0.5 * (1.0 + tanh_val) + 0.5 * preact * (1.0 - tanh_val * tanh_val) * deriv
    return value.astype(BF16), (upstream * slope).astype(BF16)


def kernel(
    inputs, out_grad, w_in, w_out,
    grad_inputs, grad_w_in, grad_w_out,
    panel, wi, wo, w_full, wo_other, part, rs_out, rs_in, rs_last, rp_out, rp_in, ah,
    g, gx_in, gy_out, gy_in, g_sent, gy_far, local_sem, *pairs,
):
    row, col = lax.axis_index("row"), lax.axis_index("col")
    y_lo, z, core = row // 16, (row // 2) % 8, row % 2
    x, y_hi = col // 4, col % 4
    other = 1 - core

    def device(y_lo=y_lo, z=z, core=core, x=x, y_hi=y_hi):
        return ((y_lo * NZ + z) * 2 + core, x * NYH + y_hi)

    twin = device(core=other)
    partner = device(y_lo=1 - y_lo)
    z_next = (device(z=(z + 1) % NZ), device(z=(z + NZ - 1) % NZ))
    z_cross = tuple(device(z=(z + d) % NZ, y_lo=1 - y_lo) for d in (1, NZ - 1))
    z_over = (device(z=(z + 2) % NZ), device(z=(z + NZ - 2) % NZ))
    x_peer = [None, *(device(x=(x + d) % NX) for d in range(1, NX))]
    y_peer = [None, *(device(y_hi=(y_hi + d) % NYH) for d in range(1, NYH))]

    sems = {kind: pairs[2 * i : 2 * i + 2] for i, kind in enumerate(SEMAPHORES)}
    sent = []

    def remote(src, dst, kind, index, to):
        send, recv = sems[kind]
        return pltpu.make_async_remote_copy(
            src_ref=src, dst_ref=dst, send_sem=send.at[index], recv_sem=recv.at[index],
            device_id=to, device_id_type=MESH,
        )

    def start(copy):
        copy.start()
        sent.append(copy)

    half_cols = pl.ds(pl.multiple_of(core * HALF, 128), HALF)
    sub = pl.ds(pl.multiple_of(y_lo * SUB, 128), SUB)
    other_sub = pl.ds(pl.multiple_of((1 - y_lo) * SUB, 128), SUB)
    other_cols = pl.ds(pl.multiple_of(other * HALF, 128), HALF)
    own = [
        pltpu.make_async_copy(inputs, panel.at[0, 0:PIECE, 0:WIDTH], local_sem.at[0]),
        pltpu.make_async_copy(out_grad, panel.at[1, 0:PIECE, 0:WIDTH], local_sem.at[1]),
        pltpu.make_async_copy(w_in.at[:, half_cols], wi.at[0:WIDTH, :], local_sem.at[2]),
        pltpu.make_async_copy(w_out.at[half_cols, :], wo.at[:, 0:WIDTH], local_sem.at[3]),
        pltpu.make_async_copy(w_in, w_full, local_sem.at[4]),
        pltpu.make_async_copy(w_out.at[other_cols, :], wo_other, local_sem.at[5]),
    ]
    for copy in own:
        copy.start()

    barrier = pltpu.get_barrier_semaphore()
    greeted = [twin, partner, *z_next, *z_cross, *z_over, *x_peer[1:], *y_peer[1:]]
    for peer in greeted:
        pl.semaphore_signal(barrier, inc=1, device_id=peer, device_id_type=MESH)
    pl.semaphore_wait(barrier, len(greeted))

    def piece_rows(dx, dy):
        slot = 4 * DY.index(dy) + dx
        return slice(slot * PIECE, (slot + 1) * PIECE)

    def piece(dx, dy, a):
        return panel.at[a, piece_rows(dx, dy), 0:WIDTH]

    def to_twin(dx, dy, a):
        there = panel.at[a, piece_rows(dx, dy), WIDTH : 2 * WIDTH]
        return remote(piece(dx, dy, a), there, "core", (a, dx, dy), twin)

    def y_copy(d, a):
        return remote(piece(0, 0, a), piece(0, NYH - d, a), "ys", (a, d // 2), y_peer[d])

    def y_forward(a):
        d = 1 if a == 0 else 3
        return remote(piece(0, NYH - d, a), piece(0, 2, a), "yf", (a,), y_peer[d])

    def x_copy(d, dy, a):
        return remote(piece(0, dy, a), piece(NX - d, dy, a), "xs", (a, d - 1, dy), x_peer[d])

    def own_ready(dy, a):
        for d in (1, 3, 2):
            start(x_copy(d, dy, a))
        start(to_twin(0, dy, a))

    def y_arrive(d, a):
        if d == 2:
            y_forward(a).wait_recv()
        else:
            y_copy(d, a).wait_recv()
            if d == (1 if a == 0 else 3):
                start(y_forward(a))
        own_ready(NYH - d, a)

    def x_arrive(dy, a):
        for d in (1, 3, 2):
            x_copy(d, dy, a).wait_recv()
            start(to_twin(NX - d, dy, a))

    def matmuls(k, a):
        for dx in range(NX):
            to_twin(dx, DY[k], a).wait_recv()
        rows = slice(k * BLOCK, (k + 1) * BLOCK)
        if a == 0:
            part[k, 0] = jnp.dot(panel[0, rows, :], wi[...], preferred_element_type=F32)
        else:
            part[k, 1] = nt(panel[1, rows, :], wo[...])

    def chunk(start):
        return pl.ds(pl.multiple_of(start, 16), CHUNK)

    def rs_copy(way, k, s, a):
        to = z_over[way] if s == 0 else z_next[way]
        return remote(
            rs_out.at[way, k, s, a], rs_in.at[way, k, s, a], "rs", (way, k, s, a), to
        )

    def rl_copy(way, cross, k, a):
        return remote(
            rs_out.at[way, k, 3, a, :, other_sub if cross else sub],
            rs_last.at[way, cross, k, a], "rl", (way, cross, k, a),
            z_cross[way] if cross else z_next[way],
        )

    def rp_copy(k, a):
        return remote(rp_out.at[k, a], rp_in.at[k, a], "rp", (k, a), partner)

    def rs_step(k, s, a):
        for way in range(2):
            if s == 0 and way != a:
                continue
            target = (z + NZ + (4 - s if way == 0 else s - 4)) % NZ
            term = part[k, a, chunk(target * CHUNK), :]
            for earlier in {2: (1, 0) if way == a else (1,), 3: (2,)}.get(s, ()):
                rs_copy(way, k, earlier, a).wait_recv()
                term = term + rs_in[way, k, earlier, a].astype(F32)
            rs_out[way, k, s, a] = term.astype(BF16)
            if s < 3:
                start(rs_copy(way, k, s, a))
            else:
                start(rl_copy(way, 1, k, a))
                start(rl_copy(way, 0, k, a))
        if s == 0:
            rp_out[k, a] = part[k, a, chunk(z * CHUNK), other_sub].astype(BF16)
            start(rp_copy(k, a))

    def ag_copy(way, k, s, a, origin):
        rows = chunk(k * BLOCK + origin * CHUNK)
        ref = ah.at[core, a, rows, sub] if s == 0 or a == 0 else ah.at[core, a, rows, :]
        to = z_over[way] if s == 3 else z_next[way]
        return remote(ref, ref, "ag", (way, k, s, a), to)

    def ag_cross(way, k, origin, cols):
        ref = ah.at[core, 1, chunk(k * BLOCK + origin * CHUNK), cols]
        return remote(ref, ref, "ac", (way, k), z_cross[way])

    def ag_partner(k, cols):
        ref = ah.at[core, 1, chunk(k * BLOCK + z * CHUNK), cols]
        return remote(ref, ref, "ap", (k,), partner)

    def act_swap(k, cols):
        ref = ah.at[core, 0, k * BLOCK : (k + 1) * BLOCK, cols]
        return remote(ref, ref, "aq", (k,), partner)

    def ag_origin(way, s):
        return (z + NZ + (-s if way == 0 else s)) % NZ

    def ag_step(k, s, a):
        for way in range(2):
            origin = ag_origin(way, s)
            if s == 0 and a == 1:
                start(ag_cross(way, k, origin, sub))
            if s > 0:
                ag_copy(way, k, s - 1, a, origin).wait_recv()
            if s == 1 and a == 1:
                ag_cross(way, k, origin, other_sub).wait_recv()
            start(ag_copy(way, k, s, a, origin))
            if s == 2 and way == a:
                start(ag_copy(way, k, 3, a, origin))
        if s == 0 and a == 1:
            start(ag_partner(k, sub))

    def gelu(k):
        sums = []
        for a in range(2):
            rp_copy(k, a).wait_recv()
            total = part[k, a, chunk(z * CHUNK), sub] + rp_in[k, a].astype(F32)
            for way in range(2):
                for cross in range(2):
                    rl_copy(way, cross, k, a).wait_recv()
                    total = total + rs_last[way, cross, k, a].astype(F32)
            sums.append(total)
        value, grad = activate(*sums)
        rows = chunk(k * BLOCK + z * CHUNK)
        ah[core, 1, rows, sub] = grad
        ag_step(k, 0, 1)
        ah[core, 0, rows, sub] = value
        ag_step(k, 0, 0)

    def half_swap(k, a, half):
        ref = ah.at[half, a, k * BLOCK : (k + 1) * BLOCK, :]
        return remote(ref, ref, "cf", (k, a), twin)

    def ag_end(k, a):
        for way in range(2):
            ag_copy(way, k, 2, a, ag_origin(way, 3)).wait_recv()
        ag_copy(a, k, 3, a, ag_origin(a, 4)).wait_recv()
        if a == 0:
            start(act_swap(k, sub))
        else:
            ag_partner(k, other_sub).wait_recv()
            start(half_swap(k, 1, core))

    def act_end(k):
        act_swap(k, other_sub).wait_recv()
        start(half_swap(k, 0, core))

    def g_piece(dx, dy):
        return g_sent.at[DY.index(dy), dx * PIECE : (dx + 1) * PIECE]

    def gx_copy(dx, dy):
        return remote(g_piece(dx, dy), gx_in.at[dx - 1, dy], "gx", (dx - 1, dy), x_peer[dx])

    def grad_block(k):
        half_swap(k, 1, other).wait_recv()
        rows = slice(k * BLOCK, (k + 1) * BLOCK)
        g[k] = nt(ah[0, 1, rows, :], w_full[:, 0:HALF]) + nt(
            ah[1, 1, rows, :], w_full[:, HALF:HIDDEN]
        )
        g_sent[k] = g[k].astype(BF16)
        for dx in (2, 1, 3):
            start(gx_copy(dx, DY[k]))

    def x_sum(dy):
        total = g[DY.index(dy), 0:PIECE]
        for dx in range(1, NX):
            gx_copy(dx, dy).wait_recv()
            total = total + gx_in[dx - 1, dy].astype(F32)
        return total

    def gy_copy(dy):
        if dy == 2:
            return remote(gy_far.at[0], gy_far.at[1], "gy", (dy - 1,), y_peer[dy])
        return remote(gy_out.at[dy - 1], gy_in.at[dy - 1], "gy", (dy - 1,), y_peer[dy])

    def y_part(dy):
        total = x_sum(dy)
        if dy == 2:
            gy_far[0] = total.astype(BF16)
        else:
            gy_out[dy - 1] = total
        start(gy_copy(dy))

    def weight_grads(a):
        for half in range(2):
            cols = slice(half * HALF, (half + 1) * HALF)
            if a == 1:
                grad_w_in[:, cols] = tn(panel[0, :, 0:WIDTH], ah[half, 1]).astype(BF16)
                continue
            if half == 0:
                for k in range(4):
                    half_swap(k, 0, other).wait_recv()
            grad_w_out[cols, :] = tn(ah[half, 0], panel[1, :, 0:WIDTH]).astype(BF16)

    for a in range(2):
        own[a].wait()
        for d in (1, 3):
            start(y_copy(d, a))
        own_ready(0, a)
    own[4].wait()
    own[5].wait()
    w_swap = [
        remote(w_full.at[:, other_cols], wi.at[WIDTH : 2 * WIDTH, :], "wx", (0,), twin),
        remote(wo_other, wo.at[:, WIDTH : 2 * WIDTH], "wx", (1,), twin),
    ]
    for copy in w_swap:
        start(copy)
    own[2].wait()
    own[3].wait()
    y_arrive(3, 0)
    x_arrive(0, 0)
    y_arrive(1, 0)
    y_arrive(3, 1)
    y_arrive(1, 1)
    x_arrive(0, 1)
    for copy in w_swap:
        copy.wait_recv()
    matmuls(0, 0)
    rs_step(0, 0, 0)
    rs_step(0, 1, 0)
    matmuls(0, 1)
    rs_step(0, 0, 1)
    rs_step(0, 1, 1)
    x_arrive(1, 0)
    y_arrive(2, 0)
    x_arrive(3, 0)
    matmuls(1, 0)
    y_arrive(2, 1)
    rs_step(1, 0, 0)
    rs_step(0, 2, 0)
    rs_step(1, 1, 0)
    x_arrive(1, 1)
    matmuls(2, 0)
    rs_step(2, 0, 0)
    rs_step(2, 1, 0)
    x_arrive(3, 1)
    matmuls(1, 1)
    rs_step(1, 0, 1)
    rs_step(1, 1, 1)
    rs_step(0, 2, 1)
    matmuls(2, 1)
    rs_step(2, 0, 1)
    rs_step(2, 1, 1)
    x_arrive(2, 0)
    matmuls(3, 0)
    rs_step(3, 0, 0)
    rs_step(0, 3, 0)
    x_arrive(2, 1)
    rs_step(1, 2, 0)
    rs_step(3, 1, 0)
    matmuls(3, 1)
    rs_step(3, 0, 1)
    rs_step(3, 1, 1)
    rs_step(1, 2, 1)
    rs_step(2, 2, 0)
    rs_step(0, 3, 1)
    rs_step(2, 2, 1)
    rs_step(1, 3, 0)
    rs_step(3, 2, 0)
    rs_step(3, 2, 1)
    rs_step(1, 3, 1)
    rs_step(2, 3, 0)
    gelu(0)
    rs_step(2, 3, 1)
    rs_step(3, 3, 0)
    rs_step(3, 3, 1)
    gelu(1)
    ag_step(0, 1, 0)
    ag_step(0, 1, 1)
    gelu(2)
    gelu(3)
    ag_step(1, 1, 0)
    ag_step(1, 1, 1)
    ag_step(0, 2, 0)
    ag_step(0, 2, 1)
    ag_step(2, 1, 0)
    ag_step(2, 1, 1)
    ag_step(3, 1, 0)
    ag_step(1, 2, 0)
    ag_step(3, 1, 1)
    ag_step(1, 2, 1)
    ag_end(0, 0)
    ag_step(2, 2, 0)
    ag_end(0, 1)
    ag_step(2, 2, 1)
    ag_step(3, 2, 0)
    grad_block(0)
    ag_end(1, 0)
    ag_step(3, 2, 1)
    ag_end(1, 1)
    ag_end(2, 0)
    act_end(0)
    grad_block(1)
    ag_end(2, 1)
    ag_end(3, 0)
    grad_block(2)
    ag_end(3, 1)
    act_end(1)
    grad_block(3)
    weight_grads(1)
    y_part(1)
    act_end(2)
    act_end(3)
    y_part(3)
    weight_grads(0)
    y_part(2)
    total = x_sum(0)
    for dy in range(1, NYH):
        gy_copy(dy).wait_recv()
        total = total + (gy_far[1].astype(F32) if dy == 2 else gy_in[dy - 1])
    grad_inputs[...] = total.astype(BF16)

    for copy in sent:
        copy.wait_send()


def store(*refs):
    half = len(refs) // 2
    sems = refs[-1]
    copies = []
    for i in range(half):
        rows = refs[i].shape[0]
        step = rows if i == 0 else rows // STORES
        for j in range(rows // step):
            part = slice(j * step, (j + 1) * step)
            copies.append(
                pltpu.make_async_copy(refs[i].at[part], refs[half + i].at[part], sems.at[i, j])
            )
    for copy in copies:
        copy.start()
    for copy in copies:
        copy.wait()


def body(inputs, out_grad, w_in, w_out):
    hbm = pl.BlockSpec(memory_space=pltpu.HBM)
    vmem = pl.BlockSpec(memory_space=pltpu.VMEM)
    dma = pltpu.SemaphoreType.DMA
    shapes = ((PIECE, WIDTH), (WIDTH, HIDDEN), (HIDDEN, WIDTH))
    results = pl.pallas_call(
        kernel,
        out_shape=tuple(pltpu.VMEM(shape, BF16) for shape in shapes),
        in_specs=[hbm] * 4,
        out_specs=(vmem,) * 3,
        scratch_shapes=[
            pltpu.VMEM((2, TOKENS, 2 * WIDTH), BF16),
            pltpu.VMEM((2 * WIDTH, HALF), BF16),
            pltpu.VMEM((HALF, 2 * WIDTH), BF16),
            pltpu.VMEM((WIDTH, HIDDEN), BF16),
            pltpu.VMEM((HALF, WIDTH), BF16),
            pltpu.VMEM((4, 2, BLOCK, HALF), F32),
            pltpu.VMEM((2, 4, 4, 2, CHUNK, HALF), BF16),
            pltpu.VMEM((2, 4, 4, 2, CHUNK, HALF), BF16),
            pltpu.VMEM((2, 2, 4, 2, CHUNK, SUB), BF16),
            pltpu.VMEM((4, 2, CHUNK, SUB), BF16),
            pltpu.VMEM((4, 2, CHUNK, SUB), BF16),
            pltpu.VMEM((2, 2, TOKENS, HALF), BF16),
            pltpu.VMEM((4, BLOCK, WIDTH), F32),
            pltpu.VMEM((3, 4, PIECE, WIDTH), BF16),
            pltpu.VMEM((3, PIECE, WIDTH), F32),
            pltpu.VMEM((3, PIECE, WIDTH), F32),
            pltpu.VMEM((4, BLOCK, WIDTH), BF16),
            pltpu.VMEM((2, PIECE, WIDTH), BF16),
            dma((6,)),
            *(dma(shape) for shape in SEMAPHORES.values() for _ in range(2)),
        ],
        compiler_params=pltpu.CompilerParams(
            collective_id=0, has_side_effects=True, vmem_limit_bytes=60 << 20
        ),
        cost_estimate=pl.CostEstimate(
            flops=6 * 10**9, bytes_accessed=5 * 10**6, transcendentals=10**6
        ),
        name="ffn_backward",
    )(inputs, out_grad, w_in, w_out)
    return pl.pallas_call(
        store,
        out_shape=tuple(jax.ShapeDtypeStruct(shape, BF16) for shape in shapes),
        in_specs=[pl.BlockSpec(memory_space=pl.ANY)] * 3,
        out_specs=(pl.BlockSpec(memory_space=pl.ANY),) * 3,
        scratch_shapes=[dma((3, STORES))],
        compiler_params=pltpu.CompilerParams(vmem_limit_bytes=1 << 20),
        name="store_results",
    )(*results)


def solution(mesh):
    return jax.shard_map(
        body,
        mesh=mesh,
        in_specs=(P("col", "row"), P("col", "row"), P("row", "col"), P("col", "row")),
        out_specs=(P("col", "row"), P("row", "col"), P("col", "row")),
        check_vma=False,
    )
```
